256 devices in a mesh: blk: 16 (over x_lo, z), head: 4 (over x_hi, core), rep: 4 (over y).
Axes of the slice: x: 4 (x_hi: 2, x_lo: 2; x = x_hi * 2 + x_lo), y: 4, z: 8, core: 2. Of those that a mesh axis runs over, the one named last changes fastest.
Arguments:
- queries: bfloat16 [8, 256, 8192], P('rep', 'blk', 'head'), parts along dimension 0, may hold values from -16 to 16
- cache_keys: bfloat16 [8, 32768, 8, 128], P('rep', 'blk', 'head'), parts along dimension 0, may hold values from -6 to 6
- cache_values: bfloat16 [8, 32768, 8, 128], P('rep', 'blk', 'head'), parts along dimension 0, may hold values from -6 to 6
- context_lengths: int32 [8], P('rep'), parts along dimension 0, may hold values from 1 to 32512, as said below
- block_order: int32 [8, 16], P('rep'), parts along dimension 0, may hold values from 0 to 15, each once within a row
Outputs:
- attended: bfloat16 [8, 256, 8192], P('rep', 'blk', 'head'), parts along dimension 0
The draws below stay inside these ranges and needn't reach their ends.
There are 4 independent parts, one for each index of `rep`. The reference program is written for one: setup_inputs(seed, part) draws one part's arguments, and reference() takes and returns one part's arrays. A program takes and returns all parts, laid end to end along the dimension named above; each array names one. Nothing has to cross between parts.
Inputs may be any that keep to these rules, and one draw needn't show every extreme that they name: `context_lengths`: in every draw some request has exactly 32512 cached positions. `block_order`: each row is a permutation of the indices along blk.
All inputs are finite; a program needn't handle non-finite values.
Results may differ from the reference program's by a relative error of at most 0.014.
Values may be sent and summed in bfloat16 or wider, within the bound.
A program may use at most 64 MiB of HBM per device.

```python
import jax
import jax.numpy as jnp
from jax import lax

Q_HEADS = 64
KV_HEADS = 8
HEAD_DIM = 128
NEW_TOKENS = 256
REQS = 2
POSITIONS = 32768
N_BLK = 16


def draw_queries(key, part):
    key = jax.random.fold_in(key, 11)
    second_key = jax.random.fold_in(key, 1)
    entries = jnp.clip(3.0 * jax.random.normal(second_key, (REQS, NEW_TOKENS, Q_HEADS, HEAD_DIM)), -15.0, 15.0)
    return entries.reshape(REQS, NEW_TOKENS, Q_HEADS * HEAD_DIM).astype(jnp.bfloat16)


def draw_cache_keys(key, part):
    key = jax.random.fold_in(key, 23)
    second_key = jax.random.fold_in(key, 1)
    entries = jnp.clip(jax.random.normal(second_key, (REQS, POSITIONS, KV_HEADS, HEAD_DIM)), -6.0, 6.0)
    return entries.astype(jnp.bfloat16)


def draw_context_lengths(key, part):
    key = jax.random.fold_in(key, 37)
    first_key, second_key = jax.random.split(key)
    longest = POSITIONS - NEW_TOKENS
    lengths = jax.random.randint(first_key, (REQS,), 1, longest + 1)
    chosen = jax.random.randint(second_key, (), 0, REQS)
    return jnp.where(jnp.arange(REQS) == chosen, longest, lengths).astype(jnp.int32)


def level_of(rng, extent, cuts, smallest, largest):
    level, own = 1.0, jax.random.fold_in(rng, 6)
    for position, blocks in cuts:
        draws = jnp.exp(jax.random.uniform(jax.random.fold_in(own, position), (blocks,), jnp.float32, smallest / len(cuts), largest / len(cuts)))
        level = level * jnp.repeat(draws, extent[position] // blocks).reshape([-1 if axis == position else 1 for axis in range(len(extent))])
    return level


def bell_draw(rng, extent, width, reach, cuts=(), kind=jnp.bfloat16):
    values = width * jax.random.normal(rng, extent, jnp.float32)
    if cuts:
        values = values * level_of(rng, extent, cuts, -0.22, 0.18)
    return jnp.clip(values, -reach, reach).astype(kind)


def setup_inputs(seed: int = 0, part: int = 0) -> dict:
    splits = jax.random.split(jax.random.key(seed), 6)
    part_keys = jax.random.split(jax.random.fold_in(splits[5], part), 6)
    return {
        "queries": draw_queries(jax.random.fold_in(jax.random.fold_in(splits[5], part), 71), part),
        "cache_keys": draw_cache_keys(jax.random.fold_in(jax.random.fold_in(splits[5], part), 71), part),
        "cache_values": bell_draw(part_keys[2], (REQS, POSITIONS, KV_HEADS, HEAD_DIM), 1.0, 6.0, ((1, 16), (2, 4))),
        "context_lengths": draw_context_lengths(jax.random.fold_in(jax.random.fold_in(splits[5], part), 71), part),
        "block_order": jax.vmap(lambda own: jax.random.permutation(own, N_BLK))(jax.random.split(part_keys[4], REQS)).reshape((REQS, N_BLK)).astype(jnp.int32),
    }


masked_score = -1.0e30


def token_positions(context_lengths, block_order):
    per_owner = NEW_TOKENS // N_BLK
    row_index = jnp.arange(NEW_TOKENS, dtype=jnp.int32)
    placed = jnp.take(block_order, row_index // per_owner, axis=1)
    return context_lengths[:, None] + placed * per_owner + (row_index % per_owner)[None, :]


def attend_pair(items):
    query_rows, key_rows, value_rows, positions = items
    scaling = HEAD_DIM ** -0.5
    scores = jnp.einsum("tgd,pd->tgp", query_rows.astype(jnp.float32), key_rows.astype(jnp.float32), precision=lax.Precision.HIGHEST) * scaling
    visible = jnp.arange(POSITIONS, dtype=jnp.int32)[None, None, :] <= positions[:, None, None]
    scores = jnp.where(visible, scores, masked_score)
    row_top = jnp.max(scores, axis=2, keepdims=True)
    weights = jnp.where(visible, jnp.exp(scores - row_top), 0.0)
    row_total = jnp.sum(weights, axis=2)
    rounded = lax.optimization_barrier(weights.astype(jnp.bfloat16))
    summed = jnp.einsum("tgp,pd->tgd", rounded.astype(jnp.float32), value_rows.astype(jnp.float32), precision=lax.Precision.HIGHEST)
    return (summed / row_total[:, :, None]).astype(jnp.bfloat16)


def reference(queries, cache_keys, cache_values, context_lengths, block_order):
    group_size = Q_HEADS // KV_HEADS
    positions = token_positions(context_lengths, block_order)
    grouped = queries.reshape(REQS, NEW_TOKENS, KV_HEADS, group_size, HEAD_DIM).transpose(0, 2, 1, 3, 4)
    grouped = grouped.reshape(REQS * KV_HEADS, NEW_TOKENS, group_size, HEAD_DIM)
    key_heads = cache_keys.transpose(0, 2, 1, 3).reshape(REQS * KV_HEADS, POSITIONS, HEAD_DIM)
    value_heads = cache_values.transpose(0, 2, 1, 3).reshape(REQS * KV_HEADS, POSITIONS, HEAD_DIM)
    position_rows = jnp.repeat(positions, KV_HEADS, axis=0)
    attended = lax.map(attend_pair, (grouped, key_heads, value_heads, position_rows))
    attended = attended.reshape(REQS, KV_HEADS, NEW_TOKENS, group_size, HEAD_DIM).transpose(0, 2, 1, 3, 4)
    return attended.reshape(REQS, NEW_TOKENS, Q_HEADS * HEAD_DIM)
```

```python
import functools

import jax
import jax.numpy as jnp
from jax import lax
from jax.experimental import pallas as pl
from jax.experimental.pallas import tpu as pltpu
from jax.sharding import PartitionSpec as P

masked_score = -1e30
lowest_top = -16384.0
MESH = pl.DeviceIdType.MESH
bf16 = jnp.bfloat16
f32 = jnp.float32

slot_column = (0, 1, 0, 0, 1, 1, 0, 0, 0, 0, 1, 1, 0, 1, 1, 1)
slot_offset = (0, 0, 1, -1, 1, -1, 2, -2, 3, -3, 2, -2, 4, 4, 3, -3)


def edge(slot, head):
    table = {
        1: (0, "x"), 2: (0, "up"), 3: (0, "down"), 4: (1, "up"), 5: (1, "down"), 6: (2, "up"), 7: (3, "down"),
        8: (6, "up"), 9: (7, "down"), 10: (6, "x"), 11: (7, "x"), 13: (12, "x"), 14: (8, "x"), 15: (9, "x"),
    }
    if slot == 12:
        return (8, "up") if head == 0 else (9, "down")
    return table[slot]


opposite = {"x": "x", "up": "down", "down": "up"}


def children(slot, head):
    return [b for b in range(1, 16) if edge(b, head)[0] == slot]


def kernel(sizes, q_ref, lengths_ref, order_ref, k_hbm, v_hbm, out_ref,
           qbuf, kraw, vraw, kp, vt, s0, s1, m0, m1, qrel, part, stats, sbuf, rbuf,
           load_sem, gsend, grecv, rsend, rrecv):
    n_z, span, tokens, group_size, dim = sizes
    rows = tokens * group_size
    scaling = dim ** -0.5 * 1.4426950408889634
    me = lax.axis_index("blk")
    column, z = lax.div(me, n_z), lax.rem(me, n_z)
    at = {
        "x": (1 - column) * n_z + z,
        "up": column * n_z + lax.rem(z + 1, n_z),
        "down": column * n_z + lax.rem(z + n_z - 1, n_z),
    }

    loads = []
    for r in range(2):
        for i, (src, dst) in enumerate(((k_hbm, kraw), (v_hbm, vraw))):
            loads.append(pltpu.make_async_copy(src.at[r], dst.at[r], load_sem.at[2 * r + i]))
            loads[-1].start()

    barrier = pltpu.get_barrier_semaphore()
    for name in ("x", "up", "down"):
        pl.semaphore_signal(barrier, inc=1, device_id={"blk": at[name]}, device_id_type=MESH)

    for r in range(2):
        for h in range(2):
            for g in range(group_size):
                begin = (h * group_size + g) * dim
                qbuf[2 * r + h, 0, pl.ds(g * tokens, tokens), :] = q_ref[r, :, pl.ds(begin, dim)]
    pl.semaphore_wait(barrier, 3)

    def gather_copy(rh, slot, head):
        parent, name = edge(slot, head)
        return pltpu.make_async_remote_copy(
            src_ref=qbuf.at[rh, parent], dst_ref=qbuf.at[rh, slot],
            send_sem=gsend.at[rh, slot], recv_sem=grecv.at[rh, slot],
            device_id={"blk": at[opposite[name]]}, device_id_type=MESH)

    def reduce_copy(rh, slot, head):
        parent, name = edge(slot, head)
        return pltpu.make_async_remote_copy(
            src_ref=sbuf.at[rh, slot], dst_ref=rbuf.at[rh, slot],
            send_sem=rsend.at[rh, slot], recv_sem=rrecv.at[rh, slot],
            device_id={"blk": at[name]}, device_id_type=MESH)

    def forward(r, slots):
        for h in range(2):
            rh = 2 * r + h
            for slot in slots:
                if slot:
                    gather_copy(rh, slot, h).wait_recv()
                for child in children(slot, h):
                    gather_copy(rh, child, h).start()

    forward(0, (0,))

    lane_token = lax.rem(lax.broadcasted_iota(jnp.int32, (1, rows), 1), tokens)
    for r in range(2):
        base = lengths_ref[r] - me * span
        for slot in range(16):
            owner_column = column if slot_column[slot] == 0 else 1 - column
            owner = owner_column * n_z + lax.rem(z + slot_offset[slot] + n_z, n_z)
            begin = base + order_ref[r, owner] * tokens
            qrel[4 * r + slot // 4, :, pl.ds(slot % 4 * rows, rows)] = lane_token + begin

    row_index = lax.broadcasted_iota(jnp.int32, (256, 256), 0)
    col_index = lax.broadcasted_iota(jnp.int32, (256, 256), 1)
    source = jnp.where(row_index < 128, 2 * row_index, 2 * row_index - 255)
    pick = jnp.where(col_index == source, 1.0, 0.0).astype(bf16)
    eye = jnp.where(row_index[:dim, :dim] == col_index[:dim, :dim], 1.0, 0.0).astype(bf16)
    ones_rows = jnp.where(lax.broadcasted_iota(jnp.int32, (16, span), 0) == 0, 1.0, 0.0).astype(bf16)

    def split_keys(r):
        def body(j, _):
            block = kraw[r, pl.ds(pl.multiple_of(j * 256, 256), 256), :]
            both = jnp.dot(pick, block, preferred_element_type=f32).astype(bf16)
            for h in range(2):
                kp[2 * r + h, pl.ds(pl.multiple_of(j * 128, 128), 128), :] = both[128 * h : 128 * h + 128]
            return 0
        lax.fori_loop(0, span // 128, body, 0, unroll=4)

    def split_values(r):
        def body(j, _):
            block = vraw[r, pl.ds(pl.multiple_of(j * 256, 256), 256), :]
            both = jnp.dot(pick, block, preferred_element_type=f32).astype(bf16)
            flipped = lax.dot_general(eye, both, (((1,), (1,)), ((), ())), preferred_element_type=f32).astype(bf16)
            for h in range(2):
                vt[2 * r + h, pl.ds(0, dim), pl.ds(pl.multiple_of(j * 128, 128), 128)] = flipped[:, 128 * h : 128 * h + 128]
            return 0
        lax.fori_loop(0, span // 128, body, 0, unroll=4)
        for h in range(2):
            vt[2 * r + h, pl.ds(dim, 16), :] = ones_rows

    def tile(t):
        r, step, h = lax.div(t, 8), lax.div(lax.rem(t, 8), 2), lax.rem(t, 2)
        return r, jnp.where(r == 0, step, 3 - step), h

    chunk = 256

    def half(following, current, s_next, m_next, s_now, m_now):
        if following is not None:
            r, g, h = tile(following)
            key_at = 2 * r + h
            q = qbuf[key_at, pl.ds(g * 4, 4)].reshape(4 * rows, dim)
            limit = qrel[4 * r + g]
            top = None
        if current is not None:
            rc, gc, hc = tile(current)
            now_at = 2 * rc + hc
            top_now = m_now[...]
            total = None
        for j in range(span // chunk):
            where = pl.ds(j * chunk, chunk)
            if following is not None:
                s = lax.dot_general(kp[key_at, where, :], q, (((1,), (1,)), ((), ())), preferred_element_type=f32)
                index = lax.broadcasted_iota(jnp.int32, (chunk, 1), 0) + j * chunk
                s = jnp.where(index <= limit, s * scaling, masked_score)
                s_next[where, :] = s
                high = jnp.max(s, axis=0, keepdims=True)
                top = high if top is None else jnp.maximum(top, high)
            if current is not None:
                w = jnp.exp2(s_now[where, :] - top_now).astype(bf16)
                x = jnp.dot(vt[now_at, :, where], w, preferred_element_type=f32)
                total = x if total is None else total + x
        if following is not None:
            m_next[...] = jnp.ceil(jnp.maximum(top, lowest_top))
        if current is not None:
            for i in range(4):
                cut = slice(i * rows, i * rows + rows)
                o = total[:dim, cut]
                top_i, sum_i = top_now[:, cut], total[dim : dim + 1, cut]
                part[now_at, gc * 4 + i] = o
                stats[now_at, gc * 4 + i] = jnp.concatenate([top_i, sum_i], axis=0)
                put(now_at, gc * 4 + i, o, top_i, sum_i)

    def put(rh, slot, o, top, total):
        sbuf[rh, slot, pl.ds(0, dim), :] = o.astype(bf16)
        row = lax.broadcasted_iota(jnp.int32, (16, rows), 0)
        top_hi = top.astype(bf16).astype(f32)
        total_hi = total.astype(bf16).astype(f32)
        tail = jnp.where(row == 0, top_hi, jnp.where(row == 1, top - top_hi, jnp.where(row == 2, total_hi, total - total_hi)))
        sbuf[rh, slot, pl.ds(dim, 16), :] = tail.astype(bf16)

    def merged(rh, slot, head):
        own = stats[rh, slot]
        tops, totals, sums = [own[0:1]], [own[1:2]], [part[rh, slot]]
        for child in children(slot, head):
            reduce_copy(rh, child, head).wait_recv()
            tail = rbuf[rh, child, pl.ds(dim, 16), :].astype(f32)
            tops.append(tail[0:1] + tail[1:2])
            totals.append(tail[2:3] + tail[3:4])
            sums.append(rbuf[rh, child, pl.ds(0, dim), :].astype(f32))
        top = functools.reduce(jnp.maximum, tops)
        factors = [jnp.exp2(x - top) for x in tops]
        total = sum(f * x for f, x in zip(factors, totals))
        o = sum(f * x for f, x in zip(factors, sums))
        return o, top, total

    def pass_on(r, slots):
        for h in range(2):
            for slot in slots:
                put(2 * r + h, slot, *merged(2 * r + h, slot, h))
                reduce_copy(2 * r + h, slot, h).start()

    def finish(r):
        for h in range(2):
            o, top, total = merged(2 * r + h, 0, h)
            result = (o / total).T.astype(bf16)
            for g in range(group_size):
                out_ref[r, :, pl.ds((h * group_size + g) * dim, dim)] = result[g * tokens : (g + 1) * tokens]

    leaves = {1: (4, 5), 2: (10, 11), 3: (13, 14, 15)}

    def send_leaves(t):
        r, g, h = tile(t)
        for group, slots in leaves.items():
            @pl.when(g == group)
            def _():
                for slot in slots:
                    reduce_copy(2 * r + h, slot, 0).start()

    def wait_gathered(r, slots):
        for h in range(2):
            for slot in slots:
                gather_copy(2 * r + h, slot, h).wait_recv()

    def after(t, static=None):
        plan = {
            0: lambda: (forward(0, (8, 9)), wait_gathered(0, (4, 5)), forward(1, (1, 2, 3))),
            1: lambda: (loads[2].wait(), split_keys(1)),
            2: lambda: (forward(0, (12,)), wait_gathered(0, (10, 11)), forward(1, (6, 7))),
            3: lambda: (loads[3].wait(), split_values(1)),
            4: lambda: (wait_gathered(0, (13, 14, 15)), forward(1, (8, 9))),
            5: lambda: (forward(1, (12,)),),
            6: lambda: (wait_gathered(1, (4, 5, 10, 11, 13, 14, 15)),),
            8: lambda: pass_on(0, (12,)),
            9: lambda: pass_on(0, (8, 9)),
            10: lambda: pass_on(0, (6, 7)),
            11: lambda: (pass_on(0, (2, 3, 1)), pass_on(1, (12,))),
            12: lambda: (pass_on(1, (8, 9)),),
            13: lambda: (finish(0), pass_on(1, (6, 7))),
        }
        if static is not None:
            if static in plan:
                plan[static]()
            return
        for when, action in plan.items():
            pl.when(t == when)(action_of(action))

    def action_of(action):
        def run():
            action()
        return run

    loads[0].wait()
    split_keys(0)
    forward(0, (1, 2, 3))
    forward(1, (0,))
    loads[1].wait()
    split_values(0)
    forward(0, (6, 7))
    half(0, None, s0, m0, None, None)

    def pair(i, _):
        t = 2 * i
        half(t + 1, t, s1, m1, s0, m0)
        send_leaves(t)
        after(t)
        half(t + 2, t + 1, s0, m0, s1, m1)
        send_leaves(t + 1)
        after(t + 1)
        return 0

    lax.fori_loop(0, 7, pair, 0)
    half(15, 14, s1, m1, s0, m0)
    half(None, 15, None, None, s1, m1)
    pass_on(1, (2, 3, 1))
    finish(1)

    def drain(slot, _):
        for rh in range(4):
            pltpu.make_async_remote_copy(
                src_ref=qbuf.at[rh, slot], dst_ref=qbuf.at[rh, slot], send_sem=gsend.at[rh, slot],
                recv_sem=grecv.at[rh, slot], device_id={"blk": at["x"]}, device_id_type=MESH).wait_send()
            pltpu.make_async_remote_copy(
                src_ref=sbuf.at[rh, slot], dst_ref=rbuf.at[rh, slot], send_sem=rsend.at[rh, slot],
                recv_sem=rrecv.at[rh, slot], device_id={"blk": at["x"]}, device_id_type=MESH).wait_send()
        return 0

    lax.fori_loop(1, 16, drain, 0)


def shards(n_blk, queries, cache_keys, cache_values, context_lengths, block_order):
    requests, tokens, width = queries.shape
    span, kv_local, dim = cache_keys.shape[1:]
    group_size = width // (kv_local * dim)
    rows = tokens * group_size
    n_z = n_blk // 2
    vmem = pl.BlockSpec(memory_space=pltpu.VMEM)
    smem = pl.BlockSpec(memory_space=pltpu.SMEM)
    hbm = pl.BlockSpec(memory_space=pl.ANY)
    keys = cache_keys.reshape(requests, span * kv_local, dim)
    values = cache_values.reshape(requests, span * kv_local, dim)
    pairs = requests * kv_local
    return pl.pallas_call(
        functools.partial(kernel, (n_z, span, tokens, group_size, dim)),
        out_shape=jax.ShapeDtypeStruct(queries.shape, bf16),
        in_specs=[vmem, smem, smem, hbm, hbm],
        out_specs=vmem,
        scratch_shapes=[
            pltpu.VMEM((pairs, 16, rows, dim), bf16),
            pltpu.VMEM((requests, span * kv_local, dim), bf16),
            pltpu.VMEM((requests, span * kv_local, dim), bf16),
            pltpu.VMEM((pairs, span, dim), bf16),
            pltpu.VMEM((pairs, dim + 16, span), bf16),
            pltpu.VMEM((span, 4 * rows), f32),
            pltpu.VMEM((span, 4 * rows), f32),
            pltpu.VMEM((1, 4 * rows), f32),
            pltpu.VMEM((1, 4 * rows), f32),
            pltpu.VMEM((requests * 4, 1, 4 * rows), jnp.int32),
            pltpu.VMEM((pairs, 16, dim, rows), f32),
            pltpu.VMEM((pairs, 16, 2, rows), f32),
            pltpu.VMEM((pairs, 16, dim + 16, rows), bf16),
            pltpu.VMEM((pairs, 16, dim + 16, rows), bf16),
            pltpu.SemaphoreType.DMA((4,)),
            pltpu.SemaphoreType.DMA((pairs, 16)),
            pltpu.SemaphoreType.DMA((pairs, 16)),
            pltpu.SemaphoreType.DMA((pairs, 16)),
            pltpu.SemaphoreType.DMA((pairs, 16)),
        ],
        compiler_params=pltpu.CompilerParams(
            collective_id=0, has_side_effects=True, vmem_limit_bytes=62 << 20
        ),
    )(queries, context_lengths, block_order, keys, values)


def solution(mesh):
    return jax.shard_map(
        functools.partial(shards, mesh.shape["blk"]),
        mesh=mesh,
        in_specs=(
            P("rep", "blk", "head"),
            P("rep", "blk", "head", None),
            P("rep", "blk", "head", None),
            P("rep"),
            P("rep", None),
        ),
        out_specs=P("rep", "blk", "head"),
        check_vma=False,
    )
```

```python
import functools

import jax
import jax.numpy as jnp
from jax import lax
from jax.experimental import pallas as pl
from jax.experimental.pallas import tpu as pltpu
from jax.sharding import PartitionSpec as P

masked_score = -1e30
lowest_top = -16384.0
MESH = pl.DeviceIdType.MESH
bf16 = jnp.bfloat16
f32 = jnp.float32

slot_column = (0, 1, 0, 0, 1, 1, 0, 0, 0, 0, 1, 1, 0, 1, 1, 1)
slot_offset = (0, 0, 1, -1, 1, -1, 2, -2, 3, -3, 2, -2, 4, 4, 3, -3)

gather_trees = ("Q", "T2")
reduce_trees = ("T2", "Q")
groups = ((5, 12, 15, 7), (11, 8, 9, 10), (4, 13, 14, 3), (6, 0, 2, 1))
tile_order = ((0, 3), (0, 1), (1, 3), (0, 0), (0, 2), (1, 1), (1, 0), (2, 3), (1, 2), (2, 0), (3, 3), (2, 2), (3, 0), (3, 2), (2, 1), (3, 1))
plan = {
    "keys": [("f", 0, 0), ("f", 1, 0)],
    "values": [],
    "first": [("f", 0, 1), ("f", 0, 6), ("f", 0, 7), ("f", 1, 1), ("w", 0, 2)],
    0: [("f", 2, 0), ("f", 3, 0), ("f", 1, 6), ("f", 1, 7), ("f", 0, 8), ("f", 0, 9), ("w", 0, 11), ("w", 0, 10)],
    1: [("f", 0, 12), ("f", 2, 1), ("f", 2, 3), ("f", 3, 1), ("f", 3, 3), ("w", 1, 2)],
    2: [("f", 1, 9), ("f", 2, 2), ("r", 0, 11), ("r", 0, 10), ("f", 3, 2), ("w", 0, 5), ("w", 0, 15)],
    3: [("f", 1, 8), ("f", 1, 12), ("w", 0, 4), ("w", 0, 13), ("w", 0, 14), ("w", 0, 3)],
    4: [("f", 2, 4), ("f", 2, 7), ("r", 0, 15), ("r", 0, 5), ("w", 1, 11), ("w", 1, 10)],
    5: [("f", 2, 6), ("r", 0, 14), ("r", 0, 13), ("f", 3, 5), ("f", 3, 6), ("f", 3, 7), ("r", 0, 4), ("w", 1, 5), ("w", 1, 15)],
    6: [("f", 2, 9), ("r", 1, 11), ("r", 1, 10)],
    7: [("f", 2, 8), ("r", 0, 9), ("r", 0, 8), ("r", 1, 15), ("w", 1, 4), ("w", 1, 13), ("w", 1, 14), ("w", 1, 3)],
    8: [("f", 2, 12), ("r", 0, 12), ("f", 3, 9), ("f", 3, 8), ("r", 2, 2), ("f", 3, 12), ("w", 2, 5), ("w", 2, 15)],
    9: [("r", 0, 1), ("r", 1, 14), ("r", 1, 13), ("r", 1, 5), ("r", 1, 4), ("r", 0, 7)],
    10: [("r", 1, 9), ("r", 2, 15), ("r", 2, 5), ("w", 2, 13), ("w", 2, 14)],
    11: [("r", 0, 6), ("r", 3, 2), ("w", 3, 15)],
    12: [("r", 0, 3), ("r", 1, 1), ("r", 2, 14), ("r", 2, 13), ("r", 2, 4), ("r", 2, 3), ("w", 3, 4), ("w", 3, 13), ("w", 3, 14)],
    13: [("r", 1, 8), ("r", 3, 15), ("r", 3, 5), ("w", 2, 11), ("w", 2, 10)],
    14: [("r", 0, 2), ("r", 1, 12), ("r", 3, 14), ("r", 3, 13), ("r", 3, 4), ("r", 3, 3), ("w", 3, 11), ("w", 3, 10)],
    15: [("r", 2, 11), ("r", 2, 10), ("r", 2, 9), ("r", 2, 8), ("r", 2, 1)],
    "last": [("r", 1, 6), ("r", 2, 12), ("r", 3, 11), ("r", 3, 10), ("r", 3, 9), ("r", 0, 0), ("r", 3, 8), ("r", 3, 1), ("r", 1, 7), ("r", 3, 12), ("r", 1, 2), ("r", 2, 7), ("r", 2, 6), ("r", 1, 3), ("r", 3, 6), ("r", 3, 7), ("r", 2, 0), ("r", 1, 0), ("r", 3, 0)],
}
split_steps = (1, 6)


def edge(tree, slot, head):
    table = {
        1: (0, "x"), 2: (0, "up"), 3: (0, "down"), 4: (1, "up"), 5: (1, "down"), 6: (2, "up"), 7: (3, "down"),
        8: (6, "up"), 9: (7, "down"), 10: (6, "x"), 11: (7, "x"), 13: (12, "x"), 14: (8, "x"), 15: (9, "x"),
        12: (6, "up2") if head == 0 else (7, "down2"),
    }
    if tree == "Q":
        table.update({6: (0, "up2"), 7: (0, "down2")})
    if tree in ("M", "M2"):
        table[12] = (8, "up") if head == 0 else (9, "down")
    if tree in ("M2", "T2"):
        table.update({10: (4, "up")} if head == 0 else {11: (5, "down")})
    return table[slot]


opposite = {"x": "x", "up": "down", "down": "up", "up2": "down2", "down2": "up2"}
place = {slot: 4 * g + i for g, slots in enumerate(groups) for i, slot in enumerate(slots)}


def children(tree, slot, head):
    return [b for b in range(1, 16) if edge(tree, b, head)[0] == slot]


def packed(values):
    return functools.reduce(lambda total, iv: total | (iv[1] << (2 * iv[0])), enumerate(values), 0)


def signed(value):
    return value - (1 << 32) if value >= 1 << 31 else value


pair_code = signed(packed([rh for rh, g in tile_order]))
group_code = signed(packed([g for rh, g in tile_order]))


def kernel(sizes, q_ref, lengths_ref, order_ref, k_hbm, v_hbm, out_ref,
           qbuf, kraw0, kraw1, vraw0, vraw1, kp, vt, s0, s1, m0, m1, qrel, part, stats, sbuf, rbuf,
           load_sem, gsend, grecv, rsend, rrecv):
    n_z, span, tokens, group_size, dim = sizes
    rows = tokens * group_size
    chunk = 256
    chunks = span // chunk
    assert chunks == 8
    scaling = dim ** -0.5 * 1.4426950408889634
    me = lax.axis_index("blk")
    column, z = lax.div(me, n_z), lax.rem(me, n_z)
    at = {
        "x": (1 - column) * n_z + z,
        "up": column * n_z + lax.rem(z + 1, n_z),
        "down": column * n_z + lax.rem(z + n_z - 1, n_z),
        "up2": column * n_z + lax.rem(z + 2, n_z),
        "down2": column * n_z + lax.rem(z + n_z - 2, n_z),
    }
    kraw, vraw = (kraw0, kraw1), (vraw0, vraw1)

    loads = []
    for r in range(2):
        for i, (src, dst) in enumerate(((k_hbm, kraw), (v_hbm, vraw))):
            loads.append(pltpu.make_async_copy(src.at[r], dst[r], load_sem.at[2 * r + i]))
            loads[-1].start()

    barrier = pltpu.get_barrier_semaphore()
    for name in at:
        pl.semaphore_signal(barrier, inc=1, device_id={"blk": at[name]}, device_id_type=MESH)

    for r in range(2):
        for h in range(2):
            for g in range(group_size):
                begin = (h * group_size + g) * dim
                qbuf[2 * r + h, place[0], pl.ds(g * tokens, tokens), :] = q_ref[r, :, pl.ds(begin, dim)]
    pl.semaphore_wait(barrier, len(at))

    def gather_copy(rh, slot):
        parent, name = edge(gather_trees[rh // 2], slot, rh % 2)
        return pltpu.make_async_remote_copy(
            src_ref=qbuf.at[rh, place[parent]], dst_ref=qbuf.at[rh, place[slot]],
            send_sem=gsend.at[rh, slot], recv_sem=grecv.at[rh, slot],
            device_id={"blk": at[opposite[name]]}, device_id_type=MESH)

    def reduce_copy(rh, slot):
        parent, name = edge(reduce_trees[rh // 2], slot, rh % 2)
        return pltpu.make_async_remote_copy(
            src_ref=sbuf.at[rh, place[slot]], dst_ref=rbuf.at[rh, slot],
            send_sem=rsend.at[rh, slot], recv_sem=rrecv.at[rh, slot],
            device_id={"blk": at[name]}, device_id_type=MESH)

    def forward(rh, slot):
        tree = gather_trees[rh // 2]
        if slot:
            gather_copy(rh, slot).wait_recv()
        for child in sorted(children(tree, slot, rh % 2), key=lambda b: -len(children(tree, b, rh % 2))):
            gather_copy(rh, child).start()

    first, limits = [], []
    lane_token = lax.rem(lax.broadcasted_iota(jnp.int32, (1, rows), 1), tokens)

    def set_positions():
        for r in range(2):
            base = lengths_ref[r] - me * span
            first.append(lax.div(jnp.clip(base, 0, span - 2 * chunk), chunk))
            limits.append(base + n_z * 2 * tokens)
            for slot in range(16):
                owner_column = column if slot_column[slot] == 0 else 1 - column
                owner = owner_column * n_z + lax.rem(z + slot_offset[slot] + n_z, n_z)
                begin = base + order_ref[r, owner] * tokens - first[r] * chunk
                qrel[4 * r + place[slot] // 4, :, pl.ds(place[slot] % 4 * rows, rows)] = lane_token + begin

    row_index = lax.broadcasted_iota(jnp.int32, (256, 256), 0)
    col_index = lax.broadcasted_iota(jnp.int32, (256, 256), 1)
    source = jnp.where(row_index < 128, 2 * row_index, 2 * row_index - 255)
    pick = jnp.where(col_index == source, 1.0, 0.0).astype(bf16)
    eye = jnp.where(row_index[:dim, :dim] == col_index[:dim, :dim], 1.0, 0.0).astype(bf16)
    sub_row = lax.broadcasted_iota(jnp.int32, (128, 1), 0)

    def rotate(r, raw):
        bits = [first[r] >> i & 1 for i in range(3)]

        def body(i, _):
            places = [pl.ds(pl.multiple_of(b * 512 + i * 64, 64), 64) for b in range(chunks)]
            blocks = [raw[p, :] for p in places]
            for level, bit in enumerate(bits):
                blocks = [jnp.where(bit == 1, blocks[(b + (1 << level)) % chunks], blocks[b]) for b in range(chunks)]
            for p, block in zip(places, blocks):
                raw[p, :] = block
            return 0

        lax.fori_loop(0, 8, body, 0)

    def split_blocks(r, raw, j):
        pieces, begins = [], []
        for i in range(4):
            block = lax.rem(first[r] + j + i // 2, chunks)
            pieces.append(raw[pl.ds(j * 512 + i * 256, 256), :])
            begins.append(block * chunk + (i % 2) * 128)
        both = jnp.dot(pick, jnp.concatenate(pieces, axis=1), preferred_element_type=f32)
        return [[both[128 * h : 128 * h + 128, 128 * i : 128 * i + 128] for i in range(4)] for h in range(2)], begins

    def split_keys(r):
        head_rows = kraw[r][pl.ds(0, 16), :].astype(f32)
        rotate(r, kraw[r])
        for j in range(0, chunks, 2):
            both, begins = split_blocks(r, kraw[r], j)
            for h in range(2):
                for i in range(4):
                    seen = sub_row + begins[i] < limits[r]
                    kp[2 * r + h, pl.ds(j * chunk + i * 128, 128), :] = jnp.where(seen, both[h][i], head_rows[h : h + 1]).astype(bf16)

    def split_values(r):
        rotate(r, vraw[r])
        for j in range(0, chunks, 2):
            both, begins = split_blocks(r, vraw[r], j)
            kept = [jnp.where(sub_row + begins[i] < limits[r], both[h][i], 0.0).astype(bf16) for h in range(2) for i in range(4)]
            flipped = lax.dot_general(eye, jnp.concatenate(kept, axis=0), (((1,), (1,)), ((), ())), preferred_element_type=f32).astype(bf16)
            for h in range(2):
                vt[2 * r + h, pl.ds(0, dim), pl.ds(j * chunk, 512)] = flipped[:, 512 * h : 512 * h + 512]
            row = lax.broadcasted_iota(jnp.int32, (16, 128), 0)
            lane = lax.broadcasted_iota(jnp.int32, (16, 128), 1)
            for i in range(4):
                counted = jnp.where((row == 0) & (lane + begins[i] < limits[r]), 1.0, 0.0).astype(bf16)
                for h in range(2):
                    vt[2 * r + h, pl.ds(dim, 16), pl.ds(j * chunk + i * 128, 128)] = counted

    def tile(t):
        t = jnp.int32(t)
        rh = jnp.int32(pair_code) >> (2 * t) & 3
        return rh, jnp.int32(group_code) >> (2 * t) & 3

    def half(following, current, s_next, m_next, s_now, m_now):
        if following is not None:
            key_at, g = tile(following)
            q = qbuf[key_at, pl.ds(g * 4, 4)].reshape(4 * rows, dim)
            limit = qrel[4 * (key_at >> 1) + g]
            top = None
        if current is not None:
            now_at, gc = tile(current)
            top_now = m_now[...]
            total = None
        for j in range(chunks):
            where = pl.ds(j * chunk, chunk)
            if following is not None:
                s = lax.dot_general(kp[key_at, where, :], q, (((1,), (1,)), ((), ())), preferred_element_type=f32) * scaling
                if j < 2:
                    index = lax.broadcasted_iota(jnp.int32, (chunk, 1), 0) + j * chunk
                    s = jnp.where(index <= limit, s, masked_score)
                s_next[where, :] = s
                high = jnp.max(s, axis=0, keepdims=True)
                top = high if top is None else jnp.maximum(top, high)
            if current is not None:
                w = jnp.exp2(s_now[where, :] - top_now).astype(bf16)
                x = jnp.dot(vt[now_at, :, where], w, preferred_element_type=f32)
                total = x if total is None else total + x
        if following is not None:
            m_next[...] = jnp.ceil(jnp.maximum(top, lowest_top))
        if current is not None:
            for i in range(4):
                cut = slice(i * rows, i * rows + rows)
                o, sum_i = total[:dim, cut], total[dim : dim + 1, cut]
                top_i = jnp.where(sum_i > 0.0, top_now[:, cut], lowest_top)
                part[now_at, gc * 4 + i] = o
                stats[now_at, gc * 4 + i] = jnp.concatenate([top_i, sum_i], axis=0)
                put(now_at, gc * 4 + i, o, top_i, sum_i)

    def put(rh, spot, o, top, total):
        sbuf[rh, spot, pl.ds(0, dim), :] = o.astype(bf16)
        row = lax.broadcasted_iota(jnp.int32, (16, rows), 0)
        top_hi = top.astype(bf16).astype(f32)
        total_hi = total.astype(bf16).astype(f32)
        tail = jnp.where(row == 0, top_hi, jnp.where(row == 1, top - top_hi, jnp.where(row == 2, total_hi, total - total_hi)))
        sbuf[rh, spot, pl.ds(dim, 16), :] = tail.astype(bf16)

    def merged(rh, slot, kids):
        own = stats[rh, place[slot]]
        tops, totals, sums = [own[0:1]], [own[1:2]], [part[rh, place[slot]]]
        for child in kids:
            reduce_copy(rh, child).wait_recv()
            tail = rbuf[rh, child, pl.ds(dim, 16), :].astype(f32)
            tops.append(tail[0:1] + tail[1:2])
            totals.append(tail[2:3] + tail[3:4])
            sums.append(rbuf[rh, child, pl.ds(0, dim), :].astype(f32))
        top = functools.reduce(jnp.maximum, tops)
        factors = [jnp.exp2(x - top) for x in tops]
        total = sum(f * x for f, x in zip(factors, totals))
        o = sum(f * x for f, x in zip(factors, sums))
        return o, top, total

    def send_back(rh, slot):
        kids = children(reduce_trees[rh // 2], slot, rh % 2)
        if slot:
            if kids:
                put(rh, place[slot], *merged(rh, slot, kids))
            reduce_copy(rh, slot).start()
            return
        o, top, total = merged(rh, slot, kids)
        result = (o / total).T.astype(bf16)
        for g in range(group_size):
            begin = (rh % 2 * group_size + g) * dim
            out_ref[rh // 2, :, pl.ds(begin, dim)] = result[g * tokens : (g + 1) * tokens]

    def act(step):
        if step in split_steps:
            i = split_steps.index(step)
            loads[2 + i].wait()
            (split_keys, split_values)[i](1)
        for kind, rh, slot in plan[step]:
            if kind == "w":
                gather_copy(rh, slot).wait_recv()
            elif kind == "f":
                forward(rh, slot)
            else:
                send_back(rh, slot)

    def act_at(t, steps):
        for step in steps:
            if plan[step] or step in split_steps:
                @pl.when(t == step)
                def _():
                    act(step)

    act("keys")
    set_positions()
    loads[0].wait()
    split_keys(0)
    act("values")
    loads[1].wait()
    split_values(0)
    act("first")
    half(0, None, s0, m0, None, None)

    def pair(i, _):
        t = 2 * i
        act_at(t, range(0, 14, 2))
        half(t + 1, t, s1, m1, s0, m0)
        act_at(t + 1, range(1, 14, 2))
        half(t + 2, t + 1, s0, m0, s1, m1)
        return 0

    lax.fori_loop(0, 7, pair, 0)
    act(14)
    half(15, 14, s1, m1, s0, m0)
    act(15)
    half(None, 15, None, None, s1, m1)
    act("last")

    def drain(slot, _):
        for rh in range(4):
            pltpu.make_async_remote_copy(
                src_ref=qbuf.at[rh, slot], dst_ref=qbuf.at[rh, slot], send_sem=gsend.at[rh, slot],
                recv_sem=grecv.at[rh, slot], device_id={"blk": at["x"]}, device_id_type=MESH).wait_send()
            pltpu.make_async_remote_copy(
                src_ref=sbuf.at[rh, slot], dst_ref=rbuf.at[rh, slot], send_sem=rsend.at[rh, slot],
                recv_sem=rrecv.at[rh, slot], device_id={"blk": at["x"]}, device_id_type=MESH).wait_send()
        return 0

    lax.fori_loop(1, 16, drain, 0)


def shards(n_blk, queries, cache_keys, cache_values, context_lengths, block_order):
    requests, tokens, width = queries.shape
    span, kv_local, dim = cache_keys.shape[1:]
    group_size = width // (kv_local * dim)
    rows = tokens * group_size
    n_z = n_blk // 2
    vmem = pl.BlockSpec(memory_space=pltpu.VMEM)
    smem = pl.BlockSpec(memory_space=pltpu.SMEM)
    hbm = pl.BlockSpec(memory_space=pl.ANY)
    keys = cache_keys.reshape(requests, span * kv_local, dim)
    values = cache_values.reshape(requests, span * kv_local, dim)
    pairs = requests * kv_local
    return pl.pallas_call(
        functools.partial(kernel, (n_z, span, tokens, group_size, dim)),
        out_shape=jax.ShapeDtypeStruct(queries.shape, bf16),
        in_specs=[vmem, smem, smem, hbm, hbm],
        out_specs=vmem,
        scratch_shapes=[
            pltpu.VMEM((pairs, 16, rows, dim), bf16),
            pltpu.VMEM((span * kv_local, dim), bf16),
            pltpu.VMEM((span * kv_local, dim), bf16),
            pltpu.VMEM((span * kv_local, dim), bf16),
            pltpu.VMEM((span * kv_local, dim), bf16),
            pltpu.VMEM((pairs, span, dim), bf16),
            pltpu.VMEM((pairs, dim + 16, span), bf16),
            pltpu.VMEM((span, 4 * rows), f32),
            pltpu.VMEM((span, 4 * rows), f32),
            pltpu.VMEM((1, 4 * rows), f32),
            pltpu.VMEM((1, 4 * rows), f32),
            pltpu.VMEM((requests * 4, 1, 4 * rows), jnp.int32),
            pltpu.VMEM((pairs, 16, dim, rows), f32),
            pltpu.VMEM((pairs, 16, 2, rows), f32),
            pltpu.VMEM((pairs, 16, dim + 16, rows), bf16),
            pltpu.VMEM((pairs, 16, dim + 16, rows), bf16),
            pltpu.SemaphoreType.DMA((4,)),
            pltpu.SemaphoreType.DMA((pairs, 16)),
            pltpu.SemaphoreType.DMA((pairs, 16)),
            pltpu.SemaphoreType.DMA((pairs, 16)),
            pltpu.SemaphoreType.DMA((pairs, 16)),
        ],
        compiler_params=pltpu.CompilerParams(
            collective_id=0, has_side_effects=True, vmem_limit_bytes=62 << 20
        ),
    )(queries, context_lengths, block_order, keys, values)


def solution(mesh):
    return jax.shard_map(
        functools.partial(shards, mesh.shape["blk"]),
        mesh=mesh,
        in_specs=(
            P("rep", "blk", "head"),
            P("rep", "blk", "head", None),
            P("rep", "blk", "head", None),
            P("rep"),
            P("rep", None),
        ),
        out_specs=P("rep", "blk", "head"),
        check_vma=False,
    )
```

```python
import functools

import jax
import jax.numpy as jnp
from jax import lax
from jax.experimental import pallas as pl
from jax.experimental.pallas import tpu as pltpu
from jax.sharding import PartitionSpec as P

masked_score = -1e30
lowest_top = -16384.0
MESH = pl.DeviceIdType.MESH
bf16 = jnp.bfloat16
f32 = jnp.float32

slot_column = (0, 1, 0, 0, 1, 1, 0, 0, 0, 0, 1, 1, 0, 1, 1, 1)
slot_offset = (0, 0, 1, -1, 1, -1, 2, -2, 3, -3, 2, -2, 4, 4, 3, -3)

gather_trees = (
    (
        ((0, "x"), (0, "up"), (0, "down"), (2, "x"), (3, "x"), (0, "up2"), (3, "down"), (6, "up"), (7, "down"), (6, "x"), (5, "down"), (8, "up"), (10, "up2"), (8, "x"), (5, "down2")),
        ((0, "x"), (0, "up"), (0, "down"), (2, "x"), (3, "x"), (2, "up"), (0, "down2"), (6, "up"), (7, "down"), (4, "up"), (7, "x"), (9, "down"), (11, "down2"), (4, "up2"), (9, "x")),
    ),
    (
        ((0, "x"), (0, "up"), (0, "down"), (1, "up"), (3, "x"), (2, "up"), (3, "down"), (6, "up"), (7, "down"), (6, "x"), (7, "x"), (6, "up2"), (12, "x"), (8, "x"), (11, "down")),
        ((0, "x"), (0, "up"), (0, "down"), (2, "x"), (1, "down"), (2, "up"), (3, "down"), (6, "up"), (7, "down"), (6, "x"), (7, "x"), (7, "down2"), (12, "x"), (10, "up"), (9, "x")),
    ),
)
reduce_trees = (
    (
        ((0, "x"), (0, "up"), (0, "down"), (1, "up"), (3, "x"), (2, "up"), (3, "down"), (6, "up"), (7, "down"), (6, "x"), (5, "down"), (8, "up"), (10, "up2"), (10, "up"), (5, "down2")),
        ((0, "x"), (0, "up"), (0, "down"), (2, "x"), (1, "down"), (2, "up"), (3, "down"), (6, "up"), (7, "down"), (4, "up"), (7, "x"), (9, "down"), (11, "down2"), (4, "up2"), (11, "down")),
    ),
    (
        ((0, "x"), (0, "up"), (0, "down"), (2, "x"), (3, "x"), (0, "up2"), (0, "down2"), (6, "up"), (7, "down"), (6, "x"), (7, "x"), (8, "up"), (10, "up2"), (8, "x"), (11, "down")),
        ((0, "x"), (0, "up"), (0, "down"), (2, "x"), (3, "x"), (0, "up2"), (0, "down2"), (6, "up"), (7, "down"), (6, "x"), (7, "x"), (9, "down"), (11, "down2"), (10, "up"), (9, "x")),
    ),
)
groups = ((13, 10, 8, 15), (5, 1, 7, 4), (3, 0, 2, 6), (11, 14, 12, 9))
tile_order = ((1, 2), (0, 2), (1, 1), (1, 3), (1, 0), (3, 1), (0, 0), (0, 3), (3, 3), (2, 3), (2, 0), (3, 0), (0, 1), (3, 2), (2, 1), (2, 2))
plan = {
    "keys": [("f", 1, 0), ("f", 0, 0), ("f", 3, 0), ("f", 2, 0)],
    "values": [],
    "first": [("f", 1, 2), ("f", 1, 7), ("f", 0, 6), ("f", 1, 3), ("f", 3, 1), ("f", 0, 2), ("f", 0, 3), ("f", 2, 1), ("f", 3, 2), ("f", 3, 3), ("f", 1, 4), ("f", 2, 2), ("f", 2, 3), ("f", 1, 11), ("f", 1, 6), ("f", 1, 9)],
    0: [("f", 0, 8), ("f", 0, 10)],
    1: [("f", 0, 5), ("f", 0, 7), ("f", 3, 6), ("f", 3, 7), ("f", 2, 7), ("w", 1, 5), ("w", 1, 1)],
    2: [("f", 2, 6), ("w", 1, 14), ("w", 1, 12)],
    3: [("f", 3, 10), ("r", 1, 5), ("w", 1, 13), ("w", 1, 10), ("w", 1, 8), ("w", 1, 15)],
    4: [("r", 1, 12), ("r", 1, 14), ("f", 2, 11), ("w", 3, 5), ("w", 3, 4)],
    5: [("f", 3, 9), ("r", 1, 15), ("r", 1, 13), ("r", 1, 10), ("r", 1, 8), ("f", 2, 8), ("w", 0, 13), ("w", 0, 15)],
    6: [("f", 3, 12), ("f", 2, 12), ("r", 3, 5), ("r", 3, 4), ("r", 3, 1), ("w", 0, 11), ("w", 0, 14), ("w", 0, 12), ("w", 0, 9)],
    7: [("r", 1, 1), ("r", 0, 13), ("r", 0, 15), ("w", 3, 11), ("w", 3, 14)],
    8: [("r", 1, 9), ("r", 0, 14), ("r", 0, 12), ("r", 0, 11), ("r", 0, 9), ("w", 2, 14), ("w", 2, 9)],
    9: [("r", 1, 6), ("r", 1, 4), ("r", 3, 14), ("r", 3, 12), ("w", 2, 13), ("w", 2, 10), ("w", 2, 15)],
    10: [("r", 1, 11), ("r", 2, 14), ("r", 2, 12), ("r", 2, 9), ("w", 3, 13), ("w", 3, 8), ("w", 3, 15)],
    11: [("r", 0, 10), ("r", 2, 15), ("r", 2, 13), ("r", 0, 8), ("w", 0, 1), ("w", 0, 4)],
    12: [("r", 1, 2), ("r", 3, 15), ("r", 3, 13), ("r", 3, 8)],
    13: [("r", 1, 7), ("r", 0, 7), ("r", 0, 5), ("r", 0, 4), ("r", 3, 10), ("r", 2, 8), ("w", 2, 5), ("w", 2, 4)],
    14: [("r", 3, 3), ("r", 3, 2), ("r", 2, 11), ("r", 2, 10)],
    15: [("r", 0, 6), ("r", 3, 11), ("r", 3, 9), ("r", 2, 5), ("r", 2, 4), ("r", 2, 1)],
    "last": [("r", 1, 3), ("r", 3, 6), ("r", 0, 3), ("r", 0, 1), ("r", 2, 7), ("r", 2, 6), ("r", 3, 7), ("r", 0, 2), ("r", 1, 0), ("r", 2, 3), ("r", 2, 2), ("r", 0, 0), ("r", 3, 0), ("r", 2, 0)],
}
split_steps = (1, 2)


def edge(tree, slot, head):
    return tree[head][slot - 1]


opposite = {"x": "x", "up": "down", "down": "up", "up2": "down2", "down2": "up2"}
place = {slot: 4 * g + i for g, slots in enumerate(groups) for i, slot in enumerate(slots)}


def children(tree, slot, head):
    return [b for b in range(1, 16) if edge(tree, b, head)[0] == slot]


def packed(values):
    return functools.reduce(lambda total, iv: total | (iv[1] << (2 * iv[0])), enumerate(values), 0)


def signed(value):
    return value - (1 << 32) if value >= 1 << 31 else value


pair_code = signed(packed([rh for rh, g in tile_order]))
group_code = signed(packed([g for rh, g in tile_order]))


def kernel(sizes, q_hbm, lengths_ref, order_ref, k_hbm, v_hbm, out_hbm,
           q_ref, out_ref, qbuf, kraw0, kraw1, vraw0, vraw1, kp, vt, s0, s1, m0, m1, qrel, part, stats, sbuf, rbuf,
           load_sem, out_sem, gsend, grecv, rsend, rrecv):
    n_z, span, tokens, group_size, dim = sizes
    rows = tokens * group_size
    chunk = 256
    chunks = span // chunk
    assert chunks == 8
    scaling = dim ** -0.5 * 1.4426950408889634
    me = lax.axis_index("blk")
    column, z = lax.div(me, n_z), lax.rem(me, n_z)
    at = {
        "x": (1 - column) * n_z + z,
        "up": column * n_z + lax.rem(z + 1, n_z),
        "down": column * n_z + lax.rem(z + n_z - 1, n_z),
        "up2": column * n_z + lax.rem(z + 2, n_z),
        "down2": column * n_z + lax.rem(z + n_z - 2, n_z),
    }
    kraw, vraw = (kraw0, kraw1), (vraw0, vraw1)

    q_load = pltpu.make_async_copy(q_hbm, q_ref, load_sem.at[4])
    q_load.start()
    loads = []
    for r in range(2):
        for i, (src, dst) in enumerate(((k_hbm, kraw), (v_hbm, vraw))):
            loads.append(pltpu.make_async_copy(src.at[r], dst[r], load_sem.at[2 * r + i]))
            loads[-1].start()

    barrier = pltpu.get_barrier_semaphore()
    for name in at:
        pl.semaphore_signal(barrier, inc=1, device_id={"blk": at[name]}, device_id_type=MESH)

    q_load.wait()
    for r in range(2):
        for h in range(2):
            for g in range(group_size):
                begin = (h * group_size + g) * dim
                qbuf[2 * r + h, place[0], pl.ds(g * tokens, tokens), :] = q_ref[r, :, pl.ds(begin, dim)]
    pl.semaphore_wait(barrier, len(at))

    def gather_copy(rh, slot):
        parent, name = edge(gather_trees[rh // 2], slot, rh % 2)
        return pltpu.make_async_remote_copy(
            src_ref=qbuf.at[rh, place[parent]], dst_ref=qbuf.at[rh, place[slot]],
            send_sem=gsend.at[rh, slot], recv_sem=grecv.at[rh, slot],
            device_id={"blk": at[opposite[name]]}, device_id_type=MESH)

    def reduce_copy(rh, slot):
        parent, name = edge(reduce_trees[rh // 2], slot, rh % 2)
        return pltpu.make_async_remote_copy(
            src_ref=sbuf.at[rh, place[slot]], dst_ref=rbuf.at[rh, slot],
            send_sem=rsend.at[rh, slot], recv_sem=rrecv.at[rh, slot],
            device_id={"blk": at[name]}, device_id_type=MESH)

    def forward(rh, slot):
        tree = gather_trees[rh // 2]
        if slot:
            gather_copy(rh, slot).wait_recv()
        for child in sorted(children(tree, slot, rh % 2), key=lambda b: -len(children(tree, b, rh % 2))):
            gather_copy(rh, child).start()

    first, limits = [], []
    lane_token = lax.rem(lax.broadcasted_iota(jnp.int32, (1, rows), 1), tokens)

    def set_positions():
        for r in range(2):
            base = lengths_ref[r] - me * span
            first.append(lax.div(jnp.clip(base, 0, span - 2 * chunk), chunk))
            limits.append(base + n_z * 2 * tokens)
            for slot in range(16):
                owner_column = column if slot_column[slot] == 0 else 1 - column
                owner = owner_column * n_z + lax.rem(z + slot_offset[slot] + n_z, n_z)
                begin = base + order_ref[r, owner] * tokens - first[r] * chunk
                qrel[4 * r + place[slot] // 4, :, pl.ds(place[slot] % 4 * rows, rows)] = lane_token + begin

    row_index = lax.broadcasted_iota(jnp.int32, (256, 256), 0)
    col_index = lax.broadcasted_iota(jnp.int32, (256, 256), 1)
    source = jnp.where(row_index < 128, 2 * row_index, 2 * row_index - 255)
    pick = jnp.where(col_index == source, 1.0, 0.0).astype(bf16)
    eye = jnp.where(row_index[:dim, :dim] == col_index[:dim, :dim], 1.0, 0.0).astype(bf16)
    sub_row = lax.broadcasted_iota(jnp.int32, (128, 1), 0)

    def rotate(r, raw):
        bits = [first[r] >> i & 1 for i in range(3)]

        def body(i, _):
            places = [pl.ds(pl.multiple_of(b * 512 + i * 64, 64), 64) for b in range(chunks)]
            blocks = [raw[p, :] for p in places]
            for level, bit in enumerate(bits):
                blocks = [jnp.where(bit == 1, blocks[(b + (1 << level)) % chunks], blocks[b]) for b in range(chunks)]
            for p, block in zip(places, blocks):
                raw[p, :] = block
            return 0

        lax.fori_loop(0, 8, body, 0)

    def split_blocks(r, raw, j):
        pieces, begins = [], []
        for i in range(4):
            block = lax.rem(first[r] + j + i // 2, chunks)
            pieces.append(raw[pl.ds(j * 512 + i * 256, 256), :])
            begins.append(block * chunk + (i % 2) * 128)
        both = jnp.dot(pick, jnp.concatenate(pieces, axis=1), preferred_element_type=f32)
        return [[both[128 * h : 128 * h + 128, 128 * i : 128 * i + 128] for i in range(4)] for h in range(2)], begins

    def split_keys(r):
        head_rows = kraw[r][pl.ds(0, 16), :].astype(f32)
        rotate(r, kraw[r])
        for j in range(0, chunks, 2):
            both, begins = split_blocks(r, kraw[r], j)
            for h in range(2):
                for i in range(4):
                    seen = sub_row + begins[i] < limits[r]
                    kp[2 * r + h, pl.ds(j * chunk + i * 128, 128), :] = jnp.where(seen, both[h][i], head_rows[h : h + 1]).astype(bf16)

    def split_values(r):
        rotate(r, vraw[r])
        for j in range(0, chunks, 2):
            both, begins = split_blocks(r, vraw[r], j)
            kept = [jnp.where(sub_row + begins[i] < limits[r], both[h][i], 0.0).astype(bf16) for h in range(2) for i in range(4)]
            flipped = lax.dot_general(eye, jnp.concatenate(kept, axis=0), (((1,), (1,)), ((), ())), preferred_element_type=f32).astype(bf16)
            for h in range(2):
                vt[2 * r + h, pl.ds(0, dim), pl.ds(j * chunk, 512)] = flipped[:, 512 * h : 512 * h + 512]
            row = lax.broadcasted_iota(jnp.int32, (16, 128), 0)
            lane = lax.broadcasted_iota(jnp.int32, (16, 128), 1)
            for i in range(4):
                counted = jnp.where((row == 0) & (lane + begins[i] < limits[r]), 1.0, 0.0).astype(bf16)
                for h in range(2):
                    vt[2 * r + h, pl.ds(dim, 16), pl.ds(j * chunk + i * 128, 128)] = counted

    def tile(t):
        t = jnp.int32(t)
        rh = jnp.int32(pair_code) >> (2 * t) & 3
        return rh, jnp.int32(group_code) >> (2 * t) & 3

    def half(following, current, s_next, m_next, s_now, m_now):
        if following is not None:
            key_at, g = tile(following)
            q = qbuf[key_at, pl.ds(g * 4, 4)].reshape(4 * rows, dim)
            limit = qrel[4 * (key_at >> 1) + g]
            top = None
        if current is not None:
            now_at, gc = tile(current)
            top_now = m_now[...]
            total = None
        for j in range(chunks):
            where = pl.ds(j * chunk, chunk)
            if following is not None:
                s = lax.dot_general(kp[key_at, where, :], q, (((1,), (1,)), ((), ())), preferred_element_type=f32) * scaling
                if j < 2:
                    index = lax.broadcasted_iota(jnp.int32, (chunk, 1), 0) + j * chunk
                    s = jnp.where(index <= limit, s, masked_score)
                s_next[where, :] = s
                high = jnp.max(s, axis=0, keepdims=True)
                top = high if top is None else jnp.maximum(top, high)
            if current is not None:
                w = jnp.exp2(s_now[where, :] - top_now).astype(bf16)
                x = jnp.dot(vt[now_at, :, where], w, preferred_element_type=f32)
                total = x if total is None else total + x
        if following is not None:
            m_next[...] = jnp.ceil(jnp.maximum(top, lowest_top))
        if current is not None:
            for i in range(4):
                cut = slice(i * rows, i * rows + rows)
                o, sum_i = total[:dim, cut], total[dim : dim + 1, cut]
                top_i = jnp.where(sum_i > 0.0, top_now[:, cut], lowest_top)
                part[now_at, gc * 4 + i] = o
                stats[now_at, gc * 4 + i] = jnp.concatenate([top_i, sum_i], axis=0)
                put(now_at, gc * 4 + i, o, top_i, sum_i)

    def put(rh, spot, o, top, total):
        sbuf[rh, spot, pl.ds(0, dim), :] = o.astype(bf16)
        row = lax.broadcasted_iota(jnp.int32, (16, rows), 0)
        top_hi = top.astype(bf16).astype(f32)
        total_hi = total.astype(bf16).astype(f32)
        tail = jnp.where(row == 0, top_hi, jnp.where(row == 1, top - top_hi, jnp.where(row == 2, total_hi, total - total_hi)))
        sbuf[rh, spot, pl.ds(dim, 16), :] = tail.astype(bf16)

    def merged(rh, slot, kids):
        own = stats[rh, place[slot]]
        tops, totals, sums = [own[0:1]], [own[1:2]], [part[rh, place[slot]]]
        for child in kids:
            reduce_copy(rh, child).wait_recv()
            tail = rbuf[rh, child, pl.ds(dim, 16), :].astype(f32)
            tops.append(tail[0:1] + tail[1:2])
            totals.append(tail[2:3] + tail[3:4])
            sums.append(rbuf[rh, child, pl.ds(0, dim), :].astype(f32))
        top = functools.reduce(jnp.maximum, tops)
        factors = [jnp.exp2(x - top) for x in tops]
        total = sum(f * x for f, x in zip(factors, totals))
        o = sum(f * x for f, x in zip(factors, sums))
        return o, top, total

    def send_back(rh, slot):
        kids = children(reduce_trees[rh // 2], slot, rh % 2)
        if slot:
            if kids:
                put(rh, place[slot], *merged(rh, slot, kids))
            reduce_copy(rh, slot).start()
            return
        o, top, total = merged(rh, slot, kids)
        result = (o / total).T.astype(bf16)
        for g in range(group_size):
            begin = (rh % 2 * group_size + g) * dim
            out_ref[rh // 2, :, pl.ds(begin, dim)] = result[g * tokens : (g + 1) * tokens]
        store(rh).start()

    def store(rh):
        where = pl.ds(rh % 2 * group_size * dim, group_size * dim)
        return pltpu.make_async_copy(out_ref.at[rh // 2, :, where], out_hbm.at[rh // 2, :, where], out_sem.at[rh])

    def drain(slot, _):
        for rh in range(4):
            pltpu.make_async_remote_copy(
                src_ref=qbuf.at[rh, slot], dst_ref=qbuf.at[rh, slot], send_sem=gsend.at[rh, slot],
                recv_sem=grecv.at[rh, slot], device_id={"blk": at["x"]}, device_id_type=MESH).wait_send()
            pltpu.make_async_remote_copy(
                src_ref=sbuf.at[rh, slot], dst_ref=rbuf.at[rh, slot], send_sem=rsend.at[rh, slot],
                recv_sem=rrecv.at[rh, slot], device_id={"blk": at["x"]}, device_id_type=MESH).wait_send()
        return 0

    def act(step):
        if step in split_steps:
            i = split_steps.index(step)
            loads[2 + i].wait()
            (split_keys, split_values)[i](1)
        for i, (kind, rh, slot) in enumerate(plan[step]):
            if step == "last" and plan[step][i:] == [("r", rh, 0)]:
                lax.fori_loop(1, 16, drain, 0)
            if kind == "w":
                gather_copy(rh, slot).wait_recv()
            elif kind == "f":
                forward(rh, slot)
            else:
                send_back(rh, slot)

    def act_at(t, steps):
        for step in steps:
            if plan[step] or step in split_steps:
                @pl.when(t == step)
                def _():
                    act(step)

    act("keys")
    set_positions()
    loads[0].wait()
    split_keys(0)
    act("values")
    loads[1].wait()
    split_values(0)
    act("first")
    half(0, None, s0, m0, None, None)

    def pair(i, _):
        t = 2 * i
        act_at(t, range(0, 14, 2))
        half(t + 1, t, s1, m1, s0, m0)
        act_at(t + 1, range(1, 14, 2))
        half(t + 2, t + 1, s0, m0, s1, m1)
        return 0

    lax.fori_loop(0, 7, pair, 0)
    act(14)
    half(15, 14, s1, m1, s0, m0)
    act(15)
    half(None, 15, None, None, s1, m1)
    act("last")

    for rh in range(4):
        store(rh).wait()


def shards(n_blk, queries, cache_keys, cache_values, context_lengths, block_order):
    requests, tokens, width = queries.shape
    span, kv_local, dim = cache_keys.shape[1:]
    group_size = width // (kv_local * dim)
    rows = tokens * group_size
    n_z = n_blk // 2
    smem = pl.BlockSpec(memory_space=pltpu.SMEM)
    hbm = pl.BlockSpec(memory_space=pl.ANY)
    keys = cache_keys.reshape(requests, span * kv_local, dim)
    values = cache_values.reshape(requests, span * kv_local, dim)
    pairs = requests * kv_local
    return pl.pallas_call(
        functools.partial(kernel, (n_z, span, tokens, group_size, dim)),
        out_shape=jax.ShapeDtypeStruct(queries.shape, bf16),
        in_specs=[hbm, smem, smem, hbm, hbm],
        out_specs=hbm,
        scratch_shapes=[
            pltpu.VMEM(queries.shape, bf16),
            pltpu.VMEM(queries.shape, bf16),
            pltpu.VMEM((pairs, 16, rows, dim), bf16),
            pltpu.VMEM((span * kv_local, dim), bf16),
            pltpu.VMEM((span * kv_local, dim), bf16),
            pltpu.VMEM((span * kv_local, dim), bf16),
            pltpu.VMEM((span * kv_local, dim), bf16),
            pltpu.VMEM((pairs, span, dim), bf16),
            pltpu.VMEM((pairs, dim + 16, span), bf16),
            pltpu.VMEM((span, 4 * rows), f32),
            pltpu.VMEM((span, 4 * rows), f32),
            pltpu.VMEM((1, 4 * rows), f32),
            pltpu.VMEM((1, 4 * rows), f32),
            pltpu.VMEM((requests * 4, 1, 4 * rows), jnp.int32),
            pltpu.VMEM((pairs, 16, dim, rows), f32),
            pltpu.VMEM((pairs, 16, 2, rows), f32),
            pltpu.VMEM((pairs, 16, dim + 16, rows), bf16),
            pltpu.VMEM((pairs, 16, dim + 16, rows), bf16),
            pltpu.SemaphoreType.DMA((5,)),
            pltpu.SemaphoreType.DMA((pairs,)),
            pltpu.SemaphoreType.DMA((pairs, 16)),
            pltpu.SemaphoreType.DMA((pairs, 16)),
            pltpu.SemaphoreType.DMA((pairs, 16)),
            pltpu.SemaphoreType.DMA((pairs, 16)),
        ],
        compiler_params=pltpu.CompilerParams(
            collective_id=0, has_side_effects=True, vmem_limit_bytes=62 << 20
        ),
    )(queries, context_lengths, block_order, keys, values)


def solution(mesh):
    return jax.shard_map(
        functools.partial(shards, mesh.shape["blk"]),
        mesh=mesh,
        in_specs=(
            P("rep", "blk", "head"),
            P("rep", "blk", "head", None),
            P("rep", "blk", "head", None),
            P("rep"),
            P("rep", None),
        ),
        out_specs=P("rep", "blk", "head"),
        check_vma=False,
    )
```

```python
import functools

import jax
import jax.numpy as jnp
from jax import lax
from jax.experimental import pallas as pl
from jax.experimental.pallas import tpu as pltpu
from jax.sharding import PartitionSpec as P

masked_score = -1e30
lowest_top = -16384.0
MESH = pl.DeviceIdType.MESH
bf16 = jnp.bfloat16
f32 = jnp.float32

slot_column = (0, 1, 0, 0, 1, 1, 0, 0, 0, 0, 1, 1, 0, 1, 1, 1)
slot_offset = (0, 0, 1, -1, 1, -1, 2, -2, 3, -3, 2, -2, 4, 4, 3, -3)

gather_trees = (
    ((0, "x"), (0, "up"), (0, "down"), (1, "up"), (3, "x"), (0, "up2"), (3, "down"), (6, "up"), (7, "down"), (6, "x"), (5, "down"), (6, "up2"), (12, "x"), (10, "up"), (9, "x")),
    ((0, "x"), (0, "up"), (0, "down"), (2, "x"), (3, "x"), (2, "up"), (3, "down"), (6, "up"), (7, "down"), (4, "up"), (7, "x"), (9, "down"), (11, "down2"), (4, "up2"), (11, "down")),
    ((0, "x"), (0, "up"), (0, "down"), (2, "x"), (3, "x"), (2, "up"), (3, "down"), (6, "up"), (7, "down"), (6, "x"), (5, "down"), (7, "down2"), (12, "x"), (4, "up2"), (9, "x")),
    ((0, "x"), (0, "up"), (0, "down"), (2, "x"), (3, "x"), (2, "up"), (3, "down"), (6, "up"), (3, "down2"), (6, "x"), (7, "x"), (9, "down"), (12, "x"), (8, "x"), (9, "x")),
)
reduce_trees = (
    ((0, "x"), (0, "up"), (0, "down"), (2, "x"), (3, "x"), (2, "up"), (3, "down"), (6, "up"), (7, "down"), (6, "x"), (5, "down"), (8, "up"), (10, "up2"), (8, "x"), (11, "down")),
    ((0, "x"), (0, "up"), (0, "down"), (2, "x"), (1, "down"), (2, "up"), (0, "down2"), (6, "up"), (7, "down"), (6, "x"), (7, "x"), (9, "down"), (15, "down"), (10, "up"), (9, "x")),
    ((0, "x"), (0, "up"), (0, "down"), (2, "x"), (3, "x"), (2, "up"), (3, "down"), (6, "up"), (7, "down"), (4, "up"), (7, "x"), (7, "down2"), (12, "x"), (10, "up"), (11, "down")),
    ((0, "x"), (0, "up"), (0, "down"), (1, "up"), (1, "down"), (0, "up2"), (0, "down2"), (6, "up"), (7, "down"), (6, "x"), (5, "down"), (6, "up2"), (14, "up"), (8, "x"), (11, "down")),
)
groups = (
    ((14, 15, 9, 13), (8, 11, 2, 4), (10, 7, 12, 6), (1, 5, 3, 0)),
    ((13, 14, 9, 7), (3, 1, 0, 2), (5, 11, 6, 4), (8, 12, 15, 10)),
    ((12, 8, 10, 11), (9, 14, 13, 15), (0, 6, 5, 4), (1, 3, 2, 7)),
    ((13, 10, 8, 5), (3, 15, 1, 7), (6, 14, 11, 12), (4, 2, 0, 9)),
)
tile_order = ((1, 1), (0, 3), (0, 2), (3, 3), (0, 1), (3, 1), (0, 0), (3, 0), (1, 0), (2, 1), (3, 2), (1, 3), (2, 0), (2, 2), (1, 2), (2, 3))
send_rank = (
    (3, 2, 3, 1, 3, 5, 1, 2, 4, 0, 0, 4, 0, 4, 4, 5),
    (5, 3, 3, 2, 0, 2, 1, 1, 4, 5, 5, 5, 1, 4, 0, 1),
    (2, 0, 5, 0, 3, 1, 2, 3, 5, 2, 1, 4, 2, 2, 0, 2),
    (0, 4, 5, 1, 3, 3, 1, 4, 2, 1, 5, 1, 3, 2, 5, 5),
)
plan = {
    "keys": [("f", 0, 0), ("f", 1, 0), ("f", 3, 0), ("f", 2, 0)],
    "values": [],
    "first": [("f", 0, 3), ("f", 0, 1), ("f", 1, 3), ("f", 0, 6), ("f", 3, 3), ("f", 2, 3), ("f", 1, 2), ("w", 1, 1)],
    0: [("f", 3, 2), ("f", 0, 7), ("f", 0, 5)],
    1: [("r", 1, 3), ("f", 2, 2), ("f", 1, 7), ("f", 0, 10), ("f", 3, 9), ("f", 0, 12)],
    2: [("f", 1, 4), ("f", 3, 7), ("f", 2, 7), ("r", 0, 1), ("f", 1, 6), ("f", 2, 5), ("f", 0, 9), ("w", 3, 4)],
    3: [("f", 1, 11), ("f", 3, 6), ("f", 3, 12), ("f", 1, 9), ("f", 2, 4), ("r", 0, 12), ("f", 2, 6), ("w", 0, 8), ("w", 0, 11), ("w", 0, 2), ("w", 0, 4)],
    4: [("r", 3, 4), ("f", 2, 9), ("r", 3, 9), ("r", 3, 2), ("w", 3, 15), ("w", 3, 1)],
    5: [("f", 2, 12), ("r", 0, 4), ("w", 0, 14), ("w", 0, 15), ("w", 0, 13)],
    6: [("r", 3, 15), ("r", 3, 3), ("f", 3, 8), ("w", 3, 13), ("w", 3, 10), ("w", 3, 5)],
    7: [("r", 0, 14), ("r", 0, 15), ("r", 0, 13), ("r", 0, 9), ("w", 1, 13), ("w", 1, 14)],
    8: [("r", 3, 13), ("r", 3, 10), ("r", 3, 7), ("w", 2, 14), ("w", 2, 13), ("w", 2, 15)],
    9: [("r", 1, 13), ("r", 1, 14), ("w", 3, 14), ("w", 3, 11)],
    10: [("r", 0, 8), ("r", 0, 10), ("r", 2, 9), ("r", 2, 14), ("r", 2, 15), ("r", 0, 11), ("r", 2, 13), ("r", 0, 7), ("w", 1, 8), ("w", 1, 12), ("w", 1, 15), ("w", 1, 10)],
    11: [("r", 3, 14), ("r", 3, 11), ("r", 3, 12), ("w", 2, 8), ("w", 2, 10), ("w", 2, 11)],
    12: [("r", 1, 8), ("r", 1, 10), ("r", 1, 15), ("r", 1, 12)],
    13: [("r", 2, 10), ("r", 2, 11), ("r", 0, 6), ("r", 2, 8), ("r", 2, 12), ("w", 1, 5)],
    14: [("r", 0, 5), ("r", 2, 5), ("r", 3, 8), ("w", 2, 1)],
    15: [("r", 1, 9), ("r", 3, 5), ("r", 1, 6), ("r", 1, 11), ("r", 1, 4), ("r", 1, 5)],
    "last": [("r", 2, 4), ("r", 2, 1), ("r", 0, 2), ("r", 2, 7), ("r", 0, 3), ("r", 2, 6), ("r", 3, 6), ("r", 1, 7), ("r", 3, 1), ("r", 1, 2), ("r", 1, 1), ("r", 2, 2), ("r", 2, 3), ("r", 0, 0), ("r", 3, 0), ("r", 1, 0), ("r", 2, 0)],
}
split_steps = ("first", 3)


def edge(tree, slot):
    return tree[slot - 1]


opposite = {"x": "x", "up": "down", "down": "up", "up2": "down2", "down2": "up2"}
place = [{slot: 4 * g + i for g, slots in enumerate(own) for i, slot in enumerate(slots)} for own in groups]


def children(tree, slot):
    return [b for b in range(1, 16) if edge(tree, b)[0] == slot]


def packed(values):
    return functools.reduce(lambda total, iv: total | (iv[1] << (2 * iv[0])), enumerate(values), 0)


def signed(value):
    return value - (1 << 32) if value >= 1 << 31 else value


pair_code = signed(packed([rh for rh, g in tile_order]))
group_code = signed(packed([g for rh, g in tile_order]))


def kernel(sizes, q_hbm, lengths_ref, order_ref, k_hbm, v_hbm, out_hbm,
           q_ref, out_ref, qbuf, kraw0, kraw1, vraw0, vraw1, kp, vt, s0, s1, m0, m1, qrel, part, stats, sbuf, rbuf,
           load_sem, out_sem, gsend, grecv, rsend, rrecv):
    n_z, span, tokens, group_size, dim = sizes
    rows = tokens * group_size
    chunk = 256
    chunks = span // chunk
    assert chunks == 8
    scaling = dim ** -0.5 * 1.4426950408889634
    me = lax.axis_index("blk")
    column, z = lax.div(me, n_z), lax.rem(me, n_z)
    at = {
        "x": (1 - column) * n_z + z,
        "up": column * n_z + lax.rem(z + 1, n_z),
        "down": column * n_z + lax.rem(z + n_z - 1, n_z),
        "up2": column * n_z + lax.rem(z + 2, n_z),
        "down2": column * n_z + lax.rem(z + n_z - 2, n_z),
    }
    kraw, vraw = (kraw0, kraw1), (vraw0, vraw1)

    q_load = pltpu.make_async_copy(q_hbm, q_ref, load_sem.at[4])
    q_load.start()
    loads = []
    for r in range(2):
        for i, (src, dst) in enumerate(((k_hbm, kraw), (v_hbm, vraw))):
            loads.append(pltpu.make_async_copy(src.at[r], dst[r], load_sem.at[2 * r + i]))
            loads[-1].start()

    barrier = pltpu.get_barrier_semaphore()
    for name in at:
        pl.semaphore_signal(barrier, inc=1, device_id={"blk": at[name]}, device_id_type=MESH)

    q_load.wait()
    for r in range(2):
        for h in range(2):
            for g in range(group_size):
                begin = (h * group_size + g) * dim
                qbuf[2 * r + h, place[2 * r + h][0], pl.ds(g * tokens, tokens), :] = q_ref[r, :, pl.ds(begin, dim)]
    pl.semaphore_wait(barrier, len(at))

    def gather_copy(rh, slot):
        parent, name = edge(gather_trees[rh], slot)
        return pltpu.make_async_remote_copy(
            src_ref=qbuf.at[rh, place[rh][parent]], dst_ref=qbuf.at[rh, place[rh][slot]],
            send_sem=gsend.at[rh, slot], recv_sem=grecv.at[rh, slot],
            device_id={"blk": at[opposite[name]]}, device_id_type=MESH)

    def reduce_copy(rh, slot):
        parent, name = edge(reduce_trees[rh], slot)
        return pltpu.make_async_remote_copy(
            src_ref=sbuf.at[rh, place[rh][slot]], dst_ref=rbuf.at[rh, slot],
            send_sem=rsend.at[rh, slot], recv_sem=rrecv.at[rh, slot],
            device_id={"blk": at[name]}, device_id_type=MESH)

    def forward(rh, slot):
        if slot:
            gather_copy(rh, slot).wait_recv()
        for child in sorted(children(gather_trees[rh], slot), key=lambda b: (send_rank[rh][b], b)):
            gather_copy(rh, child).start()

    first, limits = [], []
    lane_token = lax.rem(lax.broadcasted_iota(jnp.int32, (1, rows), 1), tokens)

    def set_positions():
        for r in range(2):
            base = lengths_ref[r] - me * span
            first.append(lax.div(jnp.clip(base, 0, span - 2 * chunk), chunk))
            limits.append(base + n_z * 2 * tokens)
            for slot in range(16):
                owner_column = column if slot_column[slot] == 0 else 1 - column
                owner = owner_column * n_z + lax.rem(z + slot_offset[slot] + n_z, n_z)
                begin = base + order_ref[r, owner] * tokens - first[r] * chunk
                for h in range(2):
                    spot = place[2 * r + h][slot]
                    qrel[4 * (2 * r + h) + spot // 4, :, pl.ds(spot % 4 * rows, rows)] = lane_token + begin

    row_index = lax.broadcasted_iota(jnp.int32, (256, 256), 0)
    col_index = lax.broadcasted_iota(jnp.int32, (256, 256), 1)
    source = jnp.where(row_index < 128, 2 * row_index, 2 * row_index - 255)
    pick = jnp.where(col_index == source, 1.0, 0.0).astype(bf16)
    eye = jnp.where(row_index[:dim, :dim] == col_index[:dim, :dim], 1.0, 0.0).astype(bf16)
    sub_row = lax.broadcasted_iota(jnp.int32, (128, 1), 0)

    def rotate(r, raw):
        bits = [first[r] >> i & 1 for i in range(3)]

        def body(i, _):
            places = [pl.ds(pl.multiple_of(b * 512 + i * 64, 64), 64) for b in range(chunks)]
            blocks = [raw[p, :] for p in places]
            for level, bit in enumerate(bits):
                blocks = [jnp.where(bit == 1, blocks[(b + (1 << level)) % chunks], blocks[b]) for b in range(chunks)]
            for p, block in zip(places, blocks):
                raw[p, :] = block
            return 0

        lax.fori_loop(0, 8, body, 0)

    def split_blocks(r, raw, j):
        pieces, begins = [], []
        for i in range(4):
            block = lax.rem(first[r] + j + i // 2, chunks)
            pieces.append(raw[pl.ds(j * 512 + i * 256, 256), :])
            begins.append(block * chunk + (i % 2) * 128)
        both = jnp.dot(pick, jnp.concatenate(pieces, axis=1), preferred_element_type=f32)
        return [[both[128 * h : 128 * h + 128, 128 * i : 128 * i + 128] for i in range(4)] for h in range(2)], begins

    def split_keys(r):
        head_rows = kraw[r][pl.ds(0, 16), :].astype(f32)
        rotate(r, kraw[r])
        for j in range(0, chunks, 2):
            both, begins = split_blocks(r, kraw[r], j)
            for h in range(2):
                for i in range(4):
                    seen = sub_row + begins[i] < limits[r]
                    kp[2 * r + h, pl.ds(j * chunk + i * 128, 128), :] = jnp.where(seen, both[h][i], head_rows[h : h + 1]).astype(bf16)

    def split_values(r):
        rotate(r, vraw[r])
        for j in range(0, chunks, 2):
            both, begins = split_blocks(r, vraw[r], j)
            kept = [jnp.where(sub_row + begins[i] < limits[r], both[h][i], 0.0).astype(bf16) for h in range(2) for i in range(4)]
            flipped = lax.dot_general(eye, jnp.concatenate(kept, axis=0), (((1,), (1,)), ((), ())), preferred_element_type=f32).astype(bf16)
            for h in range(2):
                vt[2 * r + h, pl.ds(0, dim), pl.ds(j * chunk, 512)] = flipped[:, 512 * h : 512 * h + 512]
            row = lax.broadcasted_iota(jnp.int32, (16, 128), 0)
            lane = lax.broadcasted_iota(jnp.int32, (16, 128), 1)
            for i in range(4):
                counted = jnp.where((row == 0) & (lane + begins[i] < limits[r]), 1.0, 0.0).astype(bf16)
                for h in range(2):
                    vt[2 * r + h, pl.ds(dim, 16), pl.ds(j * chunk + i * 128, 128)] = counted

    def tile(t):
        t = jnp.int32(t)
        rh = jnp.int32(pair_code) >> (2 * t) & 3
        return rh, jnp.int32(group_code) >> (2 * t) & 3

    def half(following, current, s_next, m_next, s_now, m_now):
        if following is not None:
            key_at, g = tile(following)
            q = qbuf[key_at, pl.ds(g * 4, 4)].reshape(4 * rows, dim)
            limit = qrel[4 * key_at + g]
            top = None
        if current is not None:
            now_at, gc = tile(current)
            top_now = m_now[...]
            total = None
        for j in range(chunks):
            where = pl.ds(j * chunk, chunk)
            if following is not None:
                s = lax.dot_general(kp[key_at, where, :], q, (((1,), (1,)), ((), ())), preferred_element_type=f32) * scaling
                if j < 2:
                    index = lax.broadcasted_iota(jnp.int32, (chunk, 1), 0) + j * chunk
                    s = jnp.where(index <= limit, s, masked_score)
                s_next[where, :] = s
                high = jnp.max(s, axis=0, keepdims=True)
                top = high if top is None else jnp.maximum(top, high)
            if current is not None:
                w = jnp.exp2(s_now[where, :] - top_now).astype(bf16)
                x = jnp.dot(vt[now_at, :, where], w, preferred_element_type=f32)
                total = x if total is None else total + x
        if following is not None:
            m_next[...] = jnp.ceil(jnp.maximum(top, lowest_top))
        if current is not None:
            for i in range(4):
                cut = slice(i * rows, i * rows + rows)
                o, sum_i = total[:dim, cut], total[dim : dim + 1, cut]
                top_i = jnp.where(sum_i > 0.0, top_now[:, cut], lowest_top)
                part[now_at, gc * 4 + i] = o
                stats[now_at, gc * 4 + i] = jnp.concatenate([top_i, sum_i], axis=0)
                put(now_at, gc * 4 + i, o, top_i, sum_i)

    def put(rh, spot, o, top, total):
        sbuf[rh, spot, pl.ds(0, dim), :] = o.astype(bf16)
        row = lax.broadcasted_iota(jnp.int32, (16, rows), 0)
        top_hi = top.astype(bf16).astype(f32)
        total_hi = total.astype(bf16).astype(f32)
        tail = jnp.where(row == 0, top_hi, jnp.where(row == 1, top - top_hi, jnp.where(row == 2, total_hi, total - total_hi)))
        sbuf[rh, spot, pl.ds(dim, 16), :] = tail.astype(bf16)

    def merged(rh, slot, kids):
        own = stats[rh, place[rh][slot]]
        tops, totals, sums = [own[0:1]], [own[1:2]], [part[rh, place[rh][slot]]]
        for child in kids:
            reduce_copy(rh, child).wait_recv()
            tail = rbuf[rh, child, pl.ds(dim, 16), :].astype(f32)
            tops.append(tail[0:1] + tail[1:2])
            totals.append(tail[2:3] + tail[3:4])
            sums.append(rbuf[rh, child, pl.ds(0, dim), :].astype(f32))
        top = functools.reduce(jnp.maximum, tops)
        factors = [jnp.exp2(x - top) for x in tops]
        total = sum(f * x for f, x in zip(factors, totals))
        o = sum(f * x for f, x in zip(factors, sums))
        return o, top, total

    def send_back(rh, slot):
        kids = children(reduce_trees[rh], slot)
        if slot:
            if kids:
                put(rh, place[rh][slot], *merged(rh, slot, kids))
            reduce_copy(rh, slot).start()
            return
        o, top, total = merged(rh, slot, kids)
        result = (o / total).T.astype(bf16)
        for g in range(group_size):
            begin = (rh % 2 * group_size + g) * dim
            out_ref[rh // 2, :, pl.ds(begin, dim)] = result[g * tokens : (g + 1) * tokens]
        store(rh).start()

    def store(rh):
        where = pl.ds(rh % 2 * group_size * dim, group_size * dim)
        return pltpu.make_async_copy(out_ref.at[rh // 2, :, where], out_hbm.at[rh // 2, :, where], out_sem.at[rh])

    def drain(slot, _):
        for rh in range(4):
            pltpu.make_async_remote_copy(
                src_ref=qbuf.at[rh, slot], dst_ref=qbuf.at[rh, slot], send_sem=gsend.at[rh, slot],
                recv_sem=grecv.at[rh, slot], device_id={"blk": at["x"]}, device_id_type=MESH).wait_send()
            pltpu.make_async_remote_copy(
                src_ref=sbuf.at[rh, slot], dst_ref=rbuf.at[rh, slot], send_sem=rsend.at[rh, slot],
                recv_sem=rrecv.at[rh, slot], device_id={"blk": at["x"]}, device_id_type=MESH).wait_send()
        return 0

    def act(step):
        for i, when in enumerate(split_steps):
            if step == when:
                loads[2 + i].wait()
                (split_keys, split_values)[i](1)
        for i, (kind, rh, slot) in enumerate(plan[step]):
            if step == "last" and plan[step][i:] == [("r", rh, 0)]:
                lax.fori_loop(1, 16, drain, 0)
            if kind == "w":
                gather_copy(rh, slot).wait_recv()
            elif kind == "f":
                forward(rh, slot)
            else:
                send_back(rh, slot)

    def act_at(t, steps):
        for step in steps:
            if plan[step] or step in split_steps:
                @pl.when(t == step)
                def _():
                    act(step)

    act("keys")
    set_positions()
    loads[0].wait()
    split_keys(0)
    act("values")
    loads[1].wait()
    split_values(0)
    act("first")
    half(0, None, s0, m0, None, None)

    def pair(i, _):
        t = 2 * i
        act_at(t, range(0, 14, 2))
        half(t + 1, t, s1, m1, s0, m0)
        act_at(t + 1, range(1, 14, 2))
        half(t + 2, t + 1, s0, m0, s1, m1)
        return 0

    lax.fori_loop(0, 7, pair, 0)
    act(14)
    half(15, 14, s1, m1, s0, m0)
    act(15)
    half(None, 15, None, None, s1, m1)
    act("last")

    for rh in range(4):
        store(rh).wait()


def shards(n_blk, queries, cache_keys, cache_values, context_lengths, block_order):
    requests, tokens, width = queries.shape
    span, kv_local, dim = cache_keys.shape[1:]
    group_size = width // (kv_local * dim)
    rows = tokens * group_size
    n_z = n_blk // 2
    smem = pl.BlockSpec(memory_space=pltpu.SMEM)
    hbm = pl.BlockSpec(memory_space=pl.ANY)
    keys = cache_keys.reshape(requests, span * kv_local, dim)
    values = cache_values.reshape(requests, span * kv_local, dim)
    pairs = requests * kv_local
    return pl.pallas_call(
        functools.partial(kernel, (n_z, span, tokens, group_size, dim)),
        out_shape=jax.ShapeDtypeStruct(queries.shape, bf16),
        in_specs=[hbm, smem, smem, hbm, hbm],
        out_specs=hbm,
        scratch_shapes=[
            pltpu.VMEM(queries.shape, bf16),
            pltpu.VMEM(queries.shape, bf16),
            pltpu.VMEM((pairs, 16, rows, dim), bf16),
            pltpu.VMEM((span * kv_local, dim), bf16),
            pltpu.VMEM((span * kv_local, dim), bf16),
            pltpu.VMEM((span * kv_local, dim), bf16),
            pltpu.VMEM((span * kv_local, dim), bf16),
            pltpu.VMEM((pairs, span, dim), bf16),
            pltpu.VMEM((pairs, dim + 16, span), bf16),
            pltpu.VMEM((span, 4 * rows), f32),
            pltpu.VMEM((span, 4 * rows), f32),
            pltpu.VMEM((1, 4 * rows), f32),
            pltpu.VMEM((1, 4 * rows), f32),
            pltpu.VMEM((pairs * 4, 1, 4 * rows), jnp.int32),
            pltpu.VMEM((pairs, 16, dim, rows), f32),
            pltpu.VMEM((pairs, 16, 2, rows), f32),
            pltpu.VMEM((pairs, 16, dim + 16, rows), bf16),
            pltpu.VMEM((pairs, 16, dim + 16, rows), bf16),
            pltpu.SemaphoreType.DMA((5,)),
            pltpu.SemaphoreType.DMA((pairs,)),
            pltpu.SemaphoreType.DMA((pairs, 16)),
            pltpu.SemaphoreType.DMA((pairs, 16)),
            pltpu.SemaphoreType.DMA((pairs, 16)),
            pltpu.SemaphoreType.DMA((pairs, 16)),
        ],
        compiler_params=pltpu.CompilerParams(
            collective_id=0, has_side_effects=True, vmem_limit_bytes=62 << 20
        ),
    )(queries, context_lengths, block_order, keys, values)


def solution(mesh):
    return jax.shard_map(
        functools.partial(shards, mesh.shape["blk"]),
        mesh=mesh,
        in_specs=(
            P("rep", "blk", "head"),
            P("rep", "blk", "head", None),
            P("rep", "blk", "head", None),
            P("rep"),
            P("rep", None),
        ),
        out_specs=P("rep", "blk", "head"),
        check_vma=False,
    )
```

```python
import functools

import jax
import jax.numpy as jnp
from jax import lax
from jax.experimental import pallas as pl
from jax.experimental.pallas import tpu as pltpu
from jax.sharding import PartitionSpec as P

masked_score = -1e30
lowest_top = -16384.0
MESH = pl.DeviceIdType.MESH
bf16 = jnp.bfloat16
f32 = jnp.float32

slot_column = (0, 1, 0, 0, 1, 1, 0, 0, 0, 0, 1, 1, 0, 1, 1, 1)
slot_offset = (0, 0, 1, -1, 1, -1, 2, -2, 3, -3, 2, -2, 4, 4, 3, -3)

gather_trees = (
    ((0, "x"), (0, "up"), (0, "down"), (1, "up"), (3, "x"), (0, "up2"), (3, "down"), (6, "up"), (3, "down2"), (6, "x"), (7, "x"), (8, "up"), (12, "x"), (8, "x"), (9, "x")),
    ((0, "x"), (0, "up"), (0, "down"), (2, "x"), (1, "down"), (2, "up"), (3, "down"), (2, "up2"), (7, "down"), (6, "x"), (1, "down2"), (8, "up"), (11, "down2"), (8, "x"), (11, "down")),
    ((0, "x"), (0, "up"), (0, "down"), (2, "x"), (3, "x"), (2, "up"), (0, "down2"), (6, "up"), (7, "down"), (4, "up"), (7, "x"), (9, "down"), (12, "x"), (8, "x"), (9, "x")),
    ((0, "x"), (0, "up"), (0, "down"), (1, "up"), (3, "x"), (2, "up"), (3, "down"), (6, "up"), (7, "down"), (6, "x"), (7, "x"), (7, "down2"), (12, "x"), (4, "up2"), (11, "down")),
)
reduce_trees = (
    ((0, "x"), (0, "up"), (0, "down"), (2, "x"), (1, "down"), (2, "up"), (3, "down"), (6, "up"), (3, "down2"), (6, "x"), (5, "down"), (6, "up2"), (15, "down"), (8, "x"), (5, "down2")),
    ((0, "x"), (0, "up"), (0, "down"), (2, "x"), (3, "x"), (2, "up"), (3, "down"), (6, "up"), (3, "down2"), (6, "x"), (5, "down"), (9, "down"), (12, "x"), (10, "up"), (9, "x")),
    ((0, "x"), (0, "up"), (0, "down"), (2, "x"), (1, "down"), (0, "up2"), (0, "down2"), (6, "up"), (7, "down"), (6, "x"), (7, "x"), (9, "down"), (10, "up2"), (8, "x"), (9, "x")),
    ((0, "x"), (0, "up"), (0, "down"), (1, "up"), (1, "down"), (2, "up"), (3, "down"), (6, "up"), (7, "down"), (4, "up"), (7, "x"), (9, "down"), (10, "up2"), (10, "up"), (9, "x")),
)
groups = (
    ((6, 3, 0, 2), (1, 4, 13, 8), (11, 12, 15, 14), (10, 7, 9, 5)),
    ((1, 6, 2, 5), (4, 9, 0, 3), (10, 15, 12, 8), (14, 13, 7, 11)),
    ((8, 7, 4, 1), (2, 9, 11, 10), (3, 5, 6, 0), (13, 12, 15, 14)),
    ((5, 14, 7, 10), (12, 8, 9, 0), (15, 13, 3, 11), (6, 1, 2, 4)),
)
tile_order = ((0, 0), (3, 3), (0, 3), (2, 2), (3, 1), (3, 0), (0, 2), (3, 2), (1, 3), (0, 1), (2, 3), (1, 2), (2, 0), (2, 1), (1, 1), (1, 0))
send_rank = (
    (4, 5, 4, 5, 0, 3, 1, 0, 0, 4, 1, 3, 1, 2, 5, 0),
    (1, 3, 1, 1, 1, 4, 3, 4, 1, 0, 1, 3, 3, 2, 3, 5),
    (4, 5, 2, 1, 5, 3, 2, 1, 1, 4, 3, 2, 0, 4, 4, 0),
    (4, 4, 2, 1, 1, 2, 2, 2, 3, 5, 1, 3, 0, 4, 4, 4),
)
plan = {
    "keys": [("f", 3, 0), ("f", 0, 0), ("f", 2, 0)],
    "values": [],
    "first": [("f", 3, 3), ("f", 3, 2), ("f", 3, 1), ("f", 0, 3), ("f", 0, 1), ("f", 2, 3), ("f", 0, 6), ("w", 0, 2)],
    0: [("f", 1, 0), ("f", 2, 2), ("f", 2, 7), ("f", 3, 7), ("f", 3, 6), ("f", 0, 7), ("f", 3, 4)],
    1: [("f", 0, 9), ("f", 1, 1), ("f", 1, 3), ("f", 1, 2), ("f", 0, 8), ("w", 0, 10), ("w", 0, 5)],
    2: [("f", 2, 6), ("f", 2, 4), ("f", 2, 9), ("w", 2, 5)],
    3: [("r", 0, 9), ("r", 0, 7), ("f", 3, 12), ("r", 0, 10), ("f", 3, 11), ("w", 3, 8), ("w", 3, 9)],
    4: [("r", 2, 3), ("f", 1, 11), ("r", 2, 5), ("f", 1, 8), ("w", 3, 5), ("w", 3, 14), ("w", 3, 10)],
    5: [("f", 1, 6), ("f", 1, 7), ("f", 0, 12), ("r", 3, 8), ("r", 3, 12), ("w", 0, 11), ("w", 0, 15), ("w", 0, 14)],
    6: [("r", 3, 14), ("r", 3, 5), ("f", 2, 8), ("f", 2, 12), ("w", 3, 15), ("w", 3, 13)],
    7: [("r", 0, 11), ("r", 0, 14), ("r", 0, 12), ("w", 1, 14), ("w", 1, 13)],
    8: [("r", 0, 3), ("r", 3, 13), ("r", 3, 15), ("r", 3, 11), ("w", 0, 4), ("w", 0, 13)],
    9: [("r", 1, 13), ("r", 1, 14), ("r", 1, 7), ("r", 3, 6), ("r", 1, 11), ("w", 2, 13), ("w", 2, 15), ("w", 2, 14)],
    10: [("r", 0, 13), ("r", 0, 8), ("r", 0, 4), ("w", 1, 10), ("w", 1, 15), ("w", 1, 12)],
    11: [("r", 2, 13), ("r", 3, 9), ("r", 2, 12), ("r", 2, 15), ("r", 2, 14), ("w", 2, 1)],
    12: [("r", 1, 15), ("r", 3, 10), ("r", 1, 12), ("r", 1, 8), ("r", 1, 10), ("w", 2, 11), ("w", 2, 10)],
    13: [("r", 0, 15), ("r", 2, 1), ("r", 0, 6), ("r", 3, 2), ("r", 2, 4), ("w", 1, 4), ("w", 1, 9)],
    14: [("r", 3, 7), ("r", 2, 8), ("r", 2, 10), ("r", 2, 11), ("r", 2, 9), ("w", 1, 5)],
    15: [("r", 1, 4), ("r", 3, 4), ("r", 1, 9)],
    "last": [("r", 1, 6), ("r", 1, 5), ("r", 1, 1), ("r", 0, 2), ("r", 0, 5), ("r", 2, 2), ("r", 3, 3), ("r", 2, 6), ("r", 2, 7), ("r", 3, 1), ("r", 1, 2), ("r", 1, 3), ("r", 0, 1), ("r", 3, 0), ("r", 2, 0), ("r", 1, 0), ("r", 0, 0)],
}
split_steps = ("first", 1)


def edge(tree, slot):
    return tree[slot - 1]


opposite = {"x": "x", "up": "down", "down": "up", "up2": "down2", "down2": "up2"}
place = [{slot: 4 * g + i for g, slots in enumerate(own) for i, slot in enumerate(slots)} for own in groups]


def children(tree, slot):
    return [b for b in range(1, 16) if edge(tree, b)[0] == slot]


def packed(values):
    return functools.reduce(lambda total, iv: total | (iv[1] << (2 * iv[0])), enumerate(values), 0)


def signed(value):
    return value - (1 << 32) if value >= 1 << 31 else value


pair_code = signed(packed([rh for rh, g in tile_order]))
group_code = signed(packed([g for rh, g in tile_order]))


def kernel(sizes, q_hbm, lengths_ref, order_ref, k_hbm, v_hbm, out_hbm,
           q_ref, out_ref, qbuf, kraw0, kraw1, vraw0, vraw1, kp, vt, s0, s1, m0, m1, qrel, part, stats, sbuf, rbuf,
           load_sem, out_sem, gsend, grecv, rsend, rrecv):
    n_z, span, tokens, group_size, dim = sizes
    rows = tokens * group_size
    chunk = 256
    chunks = span // chunk
    assert chunks == 8
    scaling = dim ** -0.5 * 1.4426950408889634
    me = lax.axis_index("blk")
    column, z = lax.div(me, n_z), lax.rem(me, n_z)
    at = {
        "x": (1 - column) * n_z + z,
        "up": column * n_z + lax.rem(z + 1, n_z),
        "down": column * n_z + lax.rem(z + n_z - 1, n_z),
        "up2": column * n_z + lax.rem(z + 2, n_z),
        "down2": column * n_z + lax.rem(z + n_z - 2, n_z),
    }
    kraw, vraw = (kraw0, kraw1), (vraw0, vraw1)

    q_load = pltpu.make_async_copy(q_hbm, q_ref, load_sem.at[4])
    q_load.start()
    loads = []
    for r in range(2):
        for i, (src, dst) in enumerate(((k_hbm, kraw), (v_hbm, vraw))):
            loads.append(pltpu.make_async_copy(src.at[r], dst[r], load_sem.at[2 * r + i]))
            loads[-1].start()

    barrier = pltpu.get_barrier_semaphore()
    for name in at:
        pl.semaphore_signal(barrier, inc=1, device_id={"blk": at[name]}, device_id_type=MESH)

    q_load.wait()
    for r in range(2):
        for h in range(2):
            for g in range(group_size):
                begin = (h * group_size + g) * dim
                qbuf[2 * r + h, place[2 * r + h][0], pl.ds(g * tokens, tokens), :] = q_ref[r, :, pl.ds(begin, dim)]
    pl.semaphore_wait(barrier, len(at))

    def gather_copy(rh, slot):
        parent, name = edge(gather_trees[rh], slot)
        return pltpu.make_async_remote_copy(
            src_ref=qbuf.at[rh, place[rh][parent]], dst_ref=qbuf.at[rh, place[rh][slot]],
            send_sem=gsend.at[rh, slot], recv_sem=grecv.at[rh, slot],
            device_id={"blk": at[opposite[name]]}, device_id_type=MESH)

    def reduce_copy(rh, slot):
        parent, name = edge(reduce_trees[rh], slot)
        return pltpu.make_async_remote_copy(
            src_ref=sbuf.at[rh, place[rh][slot]], dst_ref=rbuf.at[rh, slot],
            send_sem=rsend.at[rh, slot], recv_sem=rrecv.at[rh, slot],
            device_id={"blk": at[name]}, device_id_type=MESH)

    def forward(rh, slot):
        if slot:
            gather_copy(rh, slot).wait_recv()
        for child in sorted(children(gather_trees[rh], slot), key=lambda b: (send_rank[rh][b], b)):
            gather_copy(rh, child).start()

    first, limits = [], []
    lane_token = lax.rem(lax.broadcasted_iota(jnp.int32, (1, rows), 1), tokens)

    def set_positions():
        for r in range(2):
            base = lengths_ref[r] - me * span
            first.append(lax.div(jnp.clip(base, 0, span - 2 * chunk), chunk))
            limits.append(base + n_z * 2 * tokens)
            for slot in range(16):
                owner_column = column if slot_column[slot] == 0 else 1 - column
                owner = owner_column * n_z + lax.rem(z + slot_offset[slot] + n_z, n_z)
                begin = base + order_ref[r, owner] * tokens - first[r] * chunk
                for h in range(2):
                    spot = place[2 * r + h][slot]
                    qrel[4 * (2 * r + h) + spot // 4, :, pl.ds(spot % 4 * rows, rows)] = lane_token + begin

    row_index = lax.broadcasted_iota(jnp.int32, (256, 256), 0)
    col_index = lax.broadcasted_iota(jnp.int32, (256, 256), 1)
    source = jnp.where(row_index < 128, 2 * row_index, 2 * row_index - 255)
    pick = jnp.where(col_index == source, 1.0, 0.0).astype(bf16)
    eye = jnp.where(row_index[:dim, :dim] == col_index[:dim, :dim], 1.0, 0.0).astype(bf16)
    sub_row = lax.broadcasted_iota(jnp.int32, (128, 1), 0)

    def rotate(r, raw):
        bits = [first[r] >> i & 1 for i in range(3)]

        def body(i, _):
            places = [pl.ds(pl.multiple_of(b * 512 + i * 64, 64), 64) for b in range(chunks)]
            blocks = [raw[p, :] for p in places]
            for level, bit in enumerate(bits):
                blocks = [jnp.where(bit == 1, blocks[(b + (1 << level)) % chunks], blocks[b]) for b in range(chunks)]
            for p, block in zip(places, blocks):
                raw[p, :] = block
            return 0

        lax.fori_loop(0, 8, body, 0)

    def split_blocks(r, raw, j):
        pieces, begins = [], []
        for i in range(4):
            block = lax.rem(first[r] + j + i // 2, chunks)
            pieces.append(raw[pl.ds(j * 512 + i * 256, 256), :])
            begins.append(block * chunk + (i % 2) * 128)
        both = jnp.dot(pick, jnp.concatenate(pieces, axis=1), preferred_element_type=f32)
        return [[both[128 * h : 128 * h + 128, 128 * i : 128 * i + 128] for i in range(4)] for h in range(2)], begins

    def split_keys(r):
        head_rows = kraw[r][pl.ds(0, 16), :].astype(f32)
        rotate(r, kraw[r])
        for j in range(0, chunks, 2):
            both, begins = split_blocks(r, kraw[r], j)
            for h in range(2):
                for i in range(4):
                    seen = sub_row + begins[i] < limits[r]
                    kp[2 * r + h, pl.ds(j * chunk + i * 128, 128), :] = jnp.where(seen, both[h][i], head_rows[h : h + 1]).astype(bf16)

    def split_values(r):
        rotate(r, vraw[r])
        for j in range(0, chunks, 2):
            both, begins = split_blocks(r, vraw[r], j)
            kept = [jnp.where(sub_row + begins[i] < limits[r], both[h][i], 0.0).astype(bf16) for h in range(2) for i in range(4)]
            flipped = lax.dot_general(eye, jnp.concatenate(kept, axis=0), (((1,), (1,)), ((), ())), preferred_element_type=f32).astype(bf16)
            for h in range(2):
                vt[2 * r + h, pl.ds(0, dim), pl.ds(j * chunk, 512)] = flipped[:, 512 * h : 512 * h + 512]
            row = lax.broadcasted_iota(jnp.int32, (16, 128), 0)
            lane = lax.broadcasted_iota(jnp.int32, (16, 128), 1)
            for i in range(4):
                counted = jnp.where((row == 0) & (lane + begins[i] < limits[r]), 1.0, 0.0).astype(bf16)
                for h in range(2):
                    vt[2 * r + h, pl.ds(dim, 16), pl.ds(j * chunk + i * 128, 128)] = counted

    def tile(t):
        t = jnp.int32(t)
        rh = jnp.int32(pair_code) >> (2 * t) & 3
        return rh, jnp.int32(group_code) >> (2 * t) & 3

    def half(following, current, s_next, m_next, s_now, m_now):
        if following is not None:
            key_at, g = tile(following)
            q = qbuf[key_at, pl.ds(g * 4, 4)].reshape(4 * rows, dim)
            limit = qrel[4 * key_at + g]
            top = None
        if current is not None:
            now_at, gc = tile(current)
            top_now = m_now[...]
            total = None
        for j in range(chunks):
            where = pl.ds(j * chunk, chunk)
            if following is not None and j % 2 == 0:
                both = pl.ds(j * chunk, 2 * chunk)
                s = lax.dot_general(kp[key_at, both, :], q, (((1,), (1,)), ((), ())), preferred_element_type=f32) * scaling
                if j == 0:
                    index = lax.broadcasted_iota(jnp.int32, (2 * chunk, 1), 0)
                    s = jnp.where(index <= limit, s, masked_score)
                s_next[both, :] = s
                high = jnp.max(s, axis=0, keepdims=True)
                top = high if top is None else jnp.maximum(top, high)
            if current is not None:
                w = jnp.exp2(s_now[where, :] - top_now).astype(bf16)
                x = jnp.dot(vt[now_at, :, where], w, preferred_element_type=f32)
                total = x if total is None else total + x
        if following is not None:
            m_next[...] = jnp.ceil(jnp.maximum(top, lowest_top))
        if current is not None:
            for i in range(4):
                cut = slice(i * rows, i * rows + rows)
                o, sum_i = total[:dim, cut], total[dim : dim + 1, cut]
                top_i = jnp.where(sum_i > 0.0, top_now[:, cut], lowest_top)
                part[now_at, gc * 4 + i] = o
                stats[now_at, gc * 4 + i] = jnp.concatenate([top_i, sum_i], axis=0)
                put(now_at, gc * 4 + i, o, top_i, sum_i)

    def put(rh, spot, o, top, total):
        sbuf[rh, spot, pl.ds(0, dim), :] = o.astype(bf16)
        row = lax.broadcasted_iota(jnp.int32, (16, rows), 0)
        top_hi = top.astype(bf16).astype(f32)
        total_hi = total.astype(bf16).astype(f32)
        tail = jnp.where(row == 0, top_hi, jnp.where(row == 1, top - top_hi, jnp.where(row == 2, total_hi, total - total_hi)))
        sbuf[rh, spot, pl.ds(dim, 16), :] = tail.astype(bf16)

    def merged(rh, slot, kids):
        own = stats[rh, place[rh][slot]]
        tops, totals, sums = [own[0:1]], [own[1:2]], [part[rh, place[rh][slot]]]
        for child in kids:
            reduce_copy(rh, child).wait_recv()
            tail = rbuf[rh, child, pl.ds(dim, 16), :].astype(f32)
            tops.append(tail[0:1] + tail[1:2])
            totals.append(tail[2:3] + tail[3:4])
            sums.append(rbuf[rh, child, pl.ds(0, dim), :].astype(f32))
        top = functools.reduce(jnp.maximum, tops)
        factors = [jnp.exp2(x - top) for x in tops]
        total = sum(f * x for f, x in zip(factors, totals))
        o = sum(f * x for f, x in zip(factors, sums))
        return o, top, total

    def send_back(rh, slot):
        kids = children(reduce_trees[rh], slot)
        if slot:
            if kids:
                put(rh, place[rh][slot], *merged(rh, slot, kids))
            reduce_copy(rh, slot).start()
            return
        o, top, total = merged(rh, slot, kids)
        result = (o / total).T.astype(bf16)
        for g in range(group_size):
            begin = (rh % 2 * group_size + g) * dim
            out_ref[rh // 2, :, pl.ds(begin, dim)] = result[g * tokens : (g + 1) * tokens]
        store(rh).start()

    def store(rh):
        where = pl.ds(rh % 2 * group_size * dim, group_size * dim)
        return pltpu.make_async_copy(out_ref.at[rh // 2, :, where], out_hbm.at[rh // 2, :, where], out_sem.at[rh])

    def drain(slot, _):
        for rh in range(4):
            pltpu.make_async_remote_copy(
                src_ref=qbuf.at[rh, slot], dst_ref=qbuf.at[rh, slot], send_sem=gsend.at[rh, slot],
                recv_sem=grecv.at[rh, slot], device_id={"blk": at["x"]}, device_id_type=MESH).wait_send()
            pltpu.make_async_remote_copy(
                src_ref=sbuf.at[rh, slot], dst_ref=rbuf.at[rh, slot], send_sem=rsend.at[rh, slot],
                recv_sem=rrecv.at[rh, slot], device_id={"blk": at["x"]}, device_id_type=MESH).wait_send()
        return 0

    def act(step):
        for i, when in enumerate(split_steps):
            if step == when:
                loads[2 + i].wait()
                (split_keys, split_values)[i](1)
        for i, (kind, rh, slot) in enumerate(plan[step]):
            if step == "last" and plan[step][i:] == [("r", rh, 0)]:
                lax.fori_loop(1, 16, drain, 0)
            if kind == "w":
                gather_copy(rh, slot).wait_recv()
            elif kind == "f":
                forward(rh, slot)
            else:
                send_back(rh, slot)

    def act_at(t, steps):
        for step in steps:
            if plan[step] or step in split_steps:
                @pl.when(t == step)
                def _():
                    act(step)

    act("keys")
    set_positions()
    loads[0].wait()
    split_keys(0)
    act("values")
    loads[1].wait()
    split_values(0)
    act("first")
    half(0, None, s0, m0, None, None)

    def pair(i, _):
        t = 2 * i
        act_at(t, range(0, 14, 2))
        half(t + 1, t, s1, m1, s0, m0)
        act_at(t + 1, range(1, 14, 2))
        half(t + 2, t + 1, s0, m0, s1, m1)
        return 0

    lax.fori_loop(0, 7, pair, 0)
    act(14)
    half(15, 14, s1, m1, s0, m0)
    act(15)
    half(None, 15, None, None, s1, m1)
    act("last")

    for rh in range(4):
        store(rh).wait()


def shards(n_blk, queries, cache_keys, cache_values, context_lengths, block_order):
    requests, tokens, width = queries.shape
    span, kv_local, dim = cache_keys.shape[1:]
    group_size = width // (kv_local * dim)
    rows = tokens * group_size
    n_z = n_blk // 2
    smem = pl.BlockSpec(memory_space=pltpu.SMEM)
    hbm = pl.BlockSpec(memory_space=pl.ANY)
    keys = cache_keys.reshape(requests, span * kv_local, dim)
    values = cache_values.reshape(requests, span * kv_local, dim)
    pairs = requests * kv_local
    return pl.pallas_call(
        functools.partial(kernel, (n_z, span, tokens, group_size, dim)),
        out_shape=jax.ShapeDtypeStruct(queries.shape, bf16),
        in_specs=[hbm, smem, smem, hbm, hbm],
        out_specs=hbm,
        scratch_shapes=[
            pltpu.VMEM(queries.shape, bf16),
            pltpu.VMEM(queries.shape, bf16),
            pltpu.VMEM((pairs, 16, rows, dim), bf16),
            pltpu.VMEM((span * kv_local, dim), bf16),
            pltpu.VMEM((span * kv_local, dim), bf16),
            pltpu.VMEM((span * kv_local, dim), bf16),
            pltpu.VMEM((span * kv_local, dim), bf16),
            pltpu.VMEM((pairs, span, dim), bf16),
            pltpu.VMEM((pairs, dim + 16, span), bf16),
            pltpu.VMEM((span, 4 * rows), f32),
            pltpu.VMEM((span, 4 * rows), f32),
            pltpu.VMEM((1, 4 * rows), f32),
            pltpu.VMEM((1, 4 * rows), f32),
            pltpu.VMEM((pairs * 4, 1, 4 * rows), jnp.int32),
            pltpu.VMEM((pairs, 16, dim, rows), f32),
            pltpu.VMEM((pairs, 16, 2, rows), f32),
            pltpu.VMEM((pairs, 16, dim + 16, rows), bf16),
            pltpu.VMEM((pairs, 16, dim + 16, rows), bf16),
            pltpu.SemaphoreType.DMA((5,)),
            pltpu.SemaphoreType.DMA((pairs,)),
            pltpu.SemaphoreType.DMA((pairs, 16)),
            pltpu.SemaphoreType.DMA((pairs, 16)),
            pltpu.SemaphoreType.DMA((pairs, 16)),
            pltpu.SemaphoreType.DMA((pairs, 16)),
        ],
        compiler_params=pltpu.CompilerParams(
            collective_id=0, has_side_effects=True, vmem_limit_bytes=62 << 20
        ),
    )(queries, context_lengths, block_order, keys, values)


def solution(mesh):
    return jax.shard_map(
        functools.partial(shards, mesh.shape["blk"]),
        mesh=mesh,
        in_specs=(
            P("rep", "blk", "head"),
            P("rep", "blk", "head", None),
            P("rep", "blk", "head", None),
            P("rep"),
            P("rep", None),
        ),
        out_specs=P("rep", "blk", "head"),
        check_vma=False,
    )
```
